512 devices in a mesh: row: 128 (over y, z, core), samp: 4 (over x).
Axes of the slice: x: 4, y: 8, z: 8, core: 2. Of those that a mesh axis runs over, the one named last changes fastest.
Arguments:
- probe: bfloat16 [32768, 2, 512], P('row', None, 'samp'), may hold values from -6 to 6
- shift_real: float32 [32768], P('row'), may hold values from -3 to -0.5
- shift_imag: float32 [32768], P('row'), may hold values from 0.1 to 1
- child_gen: bfloat16 [65536, 128], P('row'), may hold values from -0.75 to 0.75
- child_coef: bfloat16 [2, 64, 512], P(None, None, 'samp'), may hold values from -6 to 6
- child_map: int32 [512, 128], P('row'), may hold values from -1 to 32767, as said below
- child_of: int32 [512], P('row'), may hold values from 0 to 1
- leaf_skel: int32 [128, 128], P('row'), may hold values from 0 to 511, as said below
- pair_skel: int32 [64, 128], replicated, may hold values from 0 to 255, as said below
- quad_skel: int32 [32, 128], replicated, may hold values from 0 to 255, as said below
Outputs:
- samples: float32 [32768, 2, 512], P('row', None, 'samp')
- leaf_interp: float32 [65536, 128], P('row')
- merge_interp: float32 [16384, 128], P('row')
- top_interp: float32 [8192, 128], P('row')
- top_samples: float32 [4096, 512], P('row', 'samp')
The draws below stay inside these ranges and needn't reach their ends.
Inputs may be any that keep to these rules, and one draw needn't show every extreme that they name: `child_map`: entries are front rows or -1; -1 entries stand only at the end of a block. The rows of one index of row name at most 8 rows of one leaf (rows with equal g // 256), all different; some leaf receives exactly 8 rows from every index of row. `leaf_skel`: each row holds 128 different increasing row numbers of the leaf. `pair_skel`: each row holds 128 different increasing candidate numbers. `quad_skel`: each row holds 128 different increasing candidate numbers.
All inputs are finite; a program needn't handle non-finite values.
Results may differ from the reference program's by a relative error of at most 0.0015.
Values may be sent and summed in bfloat16 or wider, within the bound.
No kernel may reach another device: no remote copies, remote signals or barrier semaphores. Data moves between devices by JAX's collectives and lax.ppermute only.
A program may use at most 64 MiB of HBM per device.

```python
import math
import jax
import jax.numpy as jnp
from jax import lax

LINE = 512
NS = 512
RANK = 128
RC = 64
BLK = 128
ROWS_DEV = 256
NF = 32768
CHILD_BLOCKS = 4
NBLK = 512
CAP = 8
N_ROW = 128


def distinct_sorted(key, count_rows, total, width):
    noise = jax.random.randint(key, (count_rows, total), 0, 1 << 16)
    scores = noise * total + jnp.arange(total)[None, :]
    picked = jnp.argsort(scores, axis=1)[:, :width]
    return jnp.sort(picked, axis=1).astype(jnp.int32)


def draw_leaf_skel(key, part):
    key = jax.random.fold_in(key, 21)
    return distinct_sorted(key, N_ROW, 2 * ROWS_DEV, RANK)


def draw_pair_skel(key, part):
    key = jax.random.fold_in(key, 22)
    return distinct_sorted(key, N_ROW // 2, 2 * RANK, RANK)


def draw_quad_skel(key, part):
    key = jax.random.fold_in(key, 23)
    return distinct_sorted(key, N_ROW // 4, 2 * RANK, RANK)


def draw_child_map(key, part):
    key = jax.random.fold_in(key, 11)
    keys = jax.random.split(key, 7)
    rows_each = CHILD_BLOCKS * BLK
    slot_total = N_ROW * CAP
    filled = jax.random.randint(keys[0], (N_ROW, CHILD_BLOCKS), 3 * BLK // 4, BLK + 1)
    is_valid = (jnp.arange(BLK)[None, None, :] < filled[:, :, None]).reshape(N_ROW, rows_each)
    busiest = jax.random.randint(keys[1], (), 0, N_ROW)
    priority = jax.random.randint(keys[2], (N_ROW,), 0, 4)
    leaf_ids = jnp.arange(N_ROW)
    priority = jnp.where((leaf_ids == busiest) | (leaf_ids == N_ROW - 1), 4, priority)
    slot_owner = jnp.arange(slot_total) // CAP
    noise = jax.random.randint(keys[3], (N_ROW, slot_total), 0, 1024)
    scores = (priority[slot_owner][None, :] * 1024 + noise) * slot_total + jnp.arange(slot_total)[None, :]
    order = jnp.argsort(-scores, axis=1)
    row_noise = jax.random.randint(keys[4], (N_ROW, rows_each), 0, 1024)
    row_scores = jnp.where(is_valid, row_noise, 2048) * rows_each + jnp.arange(rows_each)[None, :]
    ranking = jnp.argsort(jnp.argsort(row_scores, axis=1), axis=1)
    slot_taken = jnp.take_along_axis(order, jnp.minimum(ranking, slot_total - 1), axis=1)
    owners = slot_taken // CAP
    within = slot_taken % CAP
    anchor = jax.random.randint(keys[5], (N_ROW, N_ROW), 0, ROWS_DEV)
    anchor = anchor.at[0, N_ROW - 1].set(ROWS_DEV - 1)
    stride_odd = 2 * jax.random.randint(keys[6], (N_ROW, N_ROW), 0, ROWS_DEV // 2) + 1
    sources = jnp.arange(N_ROW)[:, None]
    local_rows = (anchor[sources, owners] + within * stride_odd[sources, owners]) % ROWS_DEV
    targets = jnp.where(is_valid, owners * ROWS_DEV + local_rows, -1)
    return targets.reshape(N_ROW * CHILD_BLOCKS, BLK).astype(jnp.int32)


def set_ends(drawn, own_key, low, high):
    spot = [jax.random.randint(jax.random.fold_in(own_key, axis), (), 0, length) for axis, length in enumerate(drawn.shape)]
    longest = drawn.shape.index(max(drawn.shape))
    next_to = spot[:longest] + [(spot[longest] + 1) % drawn.shape[longest]] + spot[longest + 1:]
    return drawn.at[tuple(spot)].set(low).at[tuple(next_to)].set(high)


def level_of(rng, extent, cuts, low, high):
    loudness = 1.0
    for axis_at, parts in cuts:
        draws = jax.random.uniform(jax.random.fold_in(jax.random.fold_in(rng, 6), axis_at), (parts,), jnp.float32, low / len(cuts), high / len(cuts))
        loudness = loudness * jnp.repeat(jnp.exp(draws), extent[axis_at] // parts).reshape((-1,) + (1,) * (len(extent) - 1 - axis_at))
    return loudness


def scatter_about(key, dims, scale, limit, shards=(), kind=jnp.bfloat16):
    result = scale * jax.random.normal(key, dims, jnp.float32)
    if shards:
        result = result * level_of(key, dims, shards, -0.22, 0.18)
    return jnp.clip(result, -limit, limit).astype(kind)


def setup_inputs(seed: int = 0) -> dict:
    arg_keys = jax.random.split(jax.random.key(seed), 11)
    return {
        "probe": scatter_about(arg_keys[0], (NF, 2, NS), 1.0, 6.0, ((0, 128), (2, 4))),
        "shift_real": jnp.clip(-3.0 + 2.5 * jax.random.uniform(arg_keys[1], (NF,), jnp.float32) ** level_of(arg_keys[1], (NF,), ((0, 128),), -0.2, 0.2), -3.0, -0.5),
        "shift_imag": jnp.clip(jnp.exp(math.log(1.0) - 2.3025851 * jax.random.uniform(arg_keys[2], (NF,), jnp.float32) ** level_of(arg_keys[2], (NF,), ((0, 128),), -0.2, 0.2)), 0.1, 1.0),
        "child_gen": scatter_about(arg_keys[3], (NBLK * BLK, 2 * RC), RC ** -0.5, 0.75, ((0, 128),)),
        "child_coef": scatter_about(arg_keys[4], (2, RC, NS), 1.0, 6.0, ((2, 4),)),
        "child_map": draw_child_map(jax.random.fold_in(arg_keys[10], 71), 0),
        "child_of": set_ends(jax.random.randint(arg_keys[6], (NBLK,), 0, 2), jax.random.fold_in(arg_keys[6], 1), 0, 1).astype(jnp.int32),
        "leaf_skel": draw_leaf_skel(jax.random.fold_in(arg_keys[10], 71), 0),
        "pair_skel": draw_pair_skel(jax.random.fold_in(arg_keys[10], 71), 0),
        "quad_skel": draw_quad_skel(jax.random.fold_in(arg_keys[10], 71), 0),
    }


highest = lax.Precision.HIGHEST

def interpolate(targets, chosen):
    gram_matrix = jnp.dot(chosen.astype(jnp.float32), chosen.T.astype(jnp.float32), precision=highest, preferred_element_type=jnp.float32)
    cross_terms = jnp.dot(targets.astype(jnp.float32), chosen.T.astype(jnp.float32), precision=highest, preferred_element_type=jnp.float32)
    factor = jnp.linalg.cholesky(gram_matrix)
    return jax.scipy.linalg.cho_solve((factor, True), cross_terms.T).T

def pick_rows(blocks, picks):
    return jnp.take_along_axis(blocks, picks[:, :, None], axis=1)

def reference(probe, shift_real, shift_imag, child_gen, child_coef, child_map, child_of, leaf_skel, pair_skel, quad_skel):
    total = probe.shape[0]
    centre = probe.astype(jnp.float32)
    edge_row = jnp.zeros((1, 2, NS), jnp.float32)
    plane_edge = jnp.zeros((LINE, 2, NS), jnp.float32)
    left_side = jnp.concatenate([edge_row, centre[:-1]], 0)
    right_side = jnp.concatenate([centre[1:], edge_row], 0)
    before_line = jnp.concatenate([plane_edge, centre[:-LINE]], 0)
    after_line = jnp.concatenate([centre[LINE:], plane_edge], 0)
    laplace = 4.0 * centre - left_side - right_side - before_line - after_line
    turned = jnp.stack([-centre[:, 1], centre[:, 0]], 1)
    front = laplace + shift_real[:, None, None] * centre + shift_imag[:, None, None] * turned
    rank_width = child_coef.shape[1]
    stacked = child_gen.reshape(-1, rank_width)
    is_first = jnp.repeat(child_of == 0, BLK * 2)[:, None]
    nothing = jnp.zeros_like(stacked)
    widened = jnp.concatenate([jnp.where(is_first, stacked, nothing), jnp.where(is_first, nothing, stacked)], 1)
    coef_table = child_coef.reshape(2 * rank_width, NS)
    child_values = jnp.dot(widened.astype(jnp.float32), coef_table.astype(jnp.float32), preferred_element_type=jnp.float32).reshape(-1, 2, NS).astype(jnp.bfloat16)
    targets = child_map.reshape(-1)
    places = jnp.where(targets < 0, total, targets).astype(jnp.int32)
    samples = front.at[places].add(child_values.astype(jnp.float32), mode='drop')
    leaves = samples.reshape(N_ROW, 2 * ROWS_DEV, NS)
    chosen = pick_rows(leaves, leaf_skel)
    leaf_interp = jax.vmap(interpolate)(leaves, chosen).reshape(-1, RANK)
    pair_cand = chosen.reshape(N_ROW // 2, 2 * RANK, NS)
    pair_chosen = pick_rows(pair_cand, pair_skel)
    merge_interp = jax.vmap(interpolate)(pair_cand, pair_chosen).reshape(-1, RANK)
    quad_cand = pair_chosen.reshape(N_ROW // 4, 2 * RANK, NS)
    quad_chosen = pick_rows(quad_cand, quad_skel)
    top_interp = jax.vmap(interpolate)(quad_cand, quad_chosen).reshape(-1, RANK)
    top_samples = quad_chosen.reshape(-1, NS)
    return (samples, leaf_interp, merge_interp, top_interp, top_samples)
```

```python
import functools

import jax
import jax.numpy as jnp
from jax import lax
from jax.experimental import pallas as pl
from jax.experimental.pallas import tpu as pltpu
from jax.sharding import PartitionSpec as P

LINE = 512
CAP = 8
SLOT = CAP + 2
RANK = 128
ROWS = 256
HIGHEST = lax.Precision.HIGHEST
F32 = jnp.float32
BF16 = jnp.bfloat16
VMEM_LIMIT = 48 * 1024 * 1024


def iota(shape, dim):
    return lax.broadcasted_iota(jnp.int32, shape, dim)


def column_of(row):
    square = jnp.broadcast_to(row, (128, 128))
    return jnp.sum(jnp.where(iota((128, 128), 0) == iota((128, 128), 1), square, jnp.zeros_like(square)), 1, keepdims=True)


def side_by_side(ref):
    return jnp.concatenate([ref[s] for s in range(ref.shape[0])], 1)


def dot(a, b, dims=(((1,), (0,)), ((), ())), precision=None):
    return lax.dot_general(a, b, dims, precision=precision, preferred_element_type=F32)


ROW_ROW = (((1,), (1,)), ((), ()))
COL_COL = (((0,), (0,)), ((), ()))


def route_kernel(of_ref, map_ref, gen_ref, out_ref):
    blocks = map_ref.shape[0]
    count = blocks * 128
    targets = map_ref[...]
    owner = lax.shift_right_arithmetic(targets, 8)
    place = (targets & (ROWS - 1)) + 1
    owner_row = jnp.concatenate([owner[b : b + 1] for b in range(blocks)], 1).astype(F32)
    owner_col = jnp.concatenate([column_of(owner[b : b + 1].astype(F32)) for b in range(blocks)], 0)
    place_col = jnp.concatenate([column_of(place[b : b + 1].astype(F32)) for b in range(blocks)], 0)
    label_col = jnp.concatenate([jnp.full((128, 1), of_ref[b], jnp.int32) for b in range(blocks)], 0).astype(F32)
    same = jnp.where(owner_col == owner_row, 1.0, 0.0)
    sub, lane = iota((count, count), 0), iota((count, count), 1)
    within_row = jnp.sum(jnp.where(sub < lane, same, 0.0), 0, keepdims=True)
    within_col = jnp.sum(jnp.where(lane < sub, same, 0.0), 1, keepdims=True)
    slot_row = jnp.where(owner_row >= 0, owner_row * SLOT + within_row, -1.0).astype(jnp.int32)
    info_row = jnp.where(owner_row >= 0, owner_row * SLOT + CAP, -1.0).astype(jnp.int32)
    lanes = iota((count, 128), 1)
    within_at = within_col.astype(jnp.int32)
    info = jnp.where(lanes == within_at, place_col, 0.0) + jnp.where(lanes == within_at + CAP, label_col, 0.0)
    table = jnp.concatenate([gen_ref[...], info.astype(BF16)], 0)
    rows = out_ref.shape[0]
    step = min(256, rows)
    for first in range(0, rows, step):
        at = iota((step, count), 0) + first
        pick = jnp.concatenate([jnp.where(at == slot_row, 1.0, 0.0), jnp.where(at == info_row, 1.0, 0.0)], 1)
        out_ref[first : first + step] = dot(pick.astype(BF16), table).astype(BF16)


def route(child_map, child_of, child_gen, devices):
    return pl.pallas_call(
        route_kernel,
        out_shape=jax.ShapeDtypeStruct((devices * SLOT, child_gen.shape[1]), BF16),
        in_specs=[pl.BlockSpec(memory_space=pltpu.SMEM)] + [pl.BlockSpec(memory_space=pltpu.VMEM)] * 2,
        out_specs=pl.BlockSpec(memory_space=pltpu.VMEM),
        compiler_params=pltpu.CompilerParams(vmem_limit_bytes=VMEM_LIMIT),
        name="route",
    )(child_of, child_map, child_gen)


def front_kernel(x_ref, low_ref, high_ref, left_ref, right_ref, real_ref, imag_ref, coef_ref, out_ref):
    x = x_ref[...].astype(F32)
    rows = x.shape[0]
    sub = iota(x.shape, 0)
    left, right = left_ref[...].astype(F32), right_ref[...].astype(F32)
    before = jnp.where(sub == 0, left[0:1], jnp.where(sub == 1, left[1:2], pltpu.roll(x, 2, 0)))
    after = jnp.where(
        sub == rows - 2, right[0:1], jnp.where(sub == rows - 1, right[1:2], pltpu.roll(x, rows - 2, 0))
    )
    turned = jnp.where((sub & 1) == 0, -pltpu.roll(x, rows - 1, 0), pltpu.roll(x, 1, 0))
    half = lax.shift_right_arithmetic(iota((256, 128), 0), 1) == iota((256, 128), 1)

    def spread(ref):
        blocks = [jnp.sum(jnp.where(half, ref[b : b + 1, :], 0.0), 1, keepdims=True) for b in range(ref.shape[0])]
        return jnp.concatenate(blocks, 0)

    laplace = 4.0 * x - before - after - low_ref[...].astype(F32) - high_ref[...].astype(F32)
    out_ref[0:rows] = laplace + spread(real_ref) * x + spread(imag_ref) * turned
    out_ref[rows:] = coef_ref[...].astype(F32)


def front(x, low, high, left, right, real, imag, coef):
    return pl.pallas_call(
        front_kernel,
        out_shape=jax.ShapeDtypeStruct((x.shape[0] + coef.shape[0], x.shape[1]), F32),
        in_specs=[pl.BlockSpec(memory_space=pltpu.VMEM)] * 8,
        out_specs=pl.BlockSpec(memory_space=pltpu.VMEM),
        compiler_params=pltpu.CompilerParams(vmem_limit_bytes=VMEM_LIMIT),
        name="front",
    )(x, low, high, left, right, real, imag, coef)


def leaf_kernel(where_ref, got_ref, wide_ref, skel_ref, own_ref, leaf_ref, chosen_ref):
    rows = 2 * ROWS
    got = got_ref[...]
    count = got.shape[0]
    sources = count // SLOT
    info_at = iota((sources, count), 0) * SLOT + CAP == iota((sources, count), 1)
    info = dot(jnp.where(info_at, 1.0, 0.0).astype(BF16), got).astype(BF16)
    along = iota((count, sources), 0)
    source = lax.shift_right_arithmetic(along * 6554, 16)
    spread = dot(jnp.where(source == iota((count, sources), 1), 1.0, 0.0).astype(BF16), info)
    sub = iota((count, 128), 0)
    slot = sub - SLOT * lax.shift_right_arithmetic(sub * 6554, 16)
    label = jnp.sum(jnp.where(iota((count, 128), 1) == slot + CAP, spread, 0.0), 1, keepdims=True)
    along_t = iota((sources, count), 1)
    source_t = lax.shift_right_arithmetic(along_t * 6554, 16)
    spread_t = dot(info, jnp.where(source_t == iota((sources, count), 0), 1.0, 0.0).astype(BF16), COL_COL)
    lane = iota((128, count), 1)
    slot_t = lane - SLOT * lax.shift_right_arithmetic(lane * 6554, 16)
    sub_t = iota((128, count), 0)
    code = jnp.sum(jnp.where((sub_t == slot_t) & (sub_t < CAP), spread_t, 0.0), 0, keepdims=True)
    onto = jnp.where(iota((ROWS, count), 0) + 1 == code.astype(jnp.int32), 1.0, 0.0).astype(BF16)
    wide = got.astype(F32)
    zero = jnp.zeros_like(wide)
    parts = jnp.concatenate([jnp.where(label == 0.0, wide, zero), jnp.where(label == 0.0, zero, wide)], 1).astype(BF16)
    rank = 64
    for s in range(wide_ref.shape[0]):
        coef = wide_ref[s, rows:, :].astype(BF16)
        first, second, none = coef[:rank], coef[rank:], jnp.zeros((rank, 128), BF16)
        table = jnp.concatenate(
            [jnp.concatenate([first, none, second, none], 0), jnp.concatenate([none, first, none, second], 0)], 1
        )
        values = dot(parts, table).astype(BF16)
        sums = dot(onto, values)
        for c in range(2):
            at = pl.ds(c, ROWS, stride=2)
            leaf_ref[s, at, :] = wide_ref[s, at, :] + sums[:, c * 128 : (c + 1) * 128]
    own_ref[...] = leaf_ref[where_ref[1]]
    picks = column_of(skel_ref[...].astype(F32)).astype(jnp.int32)
    chosen_ref[...] = dot(
        jnp.where(iota((RANK, rows), 1) == picks, 1.0, 0.0), side_by_side(leaf_ref), precision=HIGHEST
    )


def leaf(where, got, wide, skel):
    width = wide.shape[0] * wide.shape[2]
    return pl.pallas_call(
        leaf_kernel,
        out_shape=[
            jax.ShapeDtypeStruct((2 * ROWS, wide.shape[2]), F32),
            jax.ShapeDtypeStruct((wide.shape[0], 2 * ROWS, wide.shape[2]), F32),
            jax.ShapeDtypeStruct((RANK, width), F32),
        ],
        in_specs=[pl.BlockSpec(memory_space=pltpu.SMEM)] + [pl.BlockSpec(memory_space=pltpu.VMEM)] * 3,
        out_specs=[pl.BlockSpec(memory_space=pltpu.VMEM)] * 3,
        compiler_params=pltpu.CompilerParams(vmem_limit_bytes=VMEM_LIMIT),
        name="leaf",
    )(where, got, wide, skel)


def picked(skel_ref, group, low, own, other):
    picks = column_of(skel_ref[pl.ds(group, 1), :].astype(F32)).astype(jnp.int32)
    lane = iota((RANK, RANK), 1)
    onto_own = jnp.where(lane + RANK * low == picks, 1.0, 0.0)
    onto_other = jnp.where(lane + RANK * (1 - low) == picks, 1.0, 0.0)
    return dot(jnp.concatenate([onto_own, onto_other], 1), jnp.concatenate([own, other], 0), precision=HIGHEST)


def pair_kernel(where_ref, own_ref, other_ref, skel_ref, out_ref):
    position = where_ref[0]
    group, low = lax.shift_right_arithmetic(position, 1), position & 1
    out_ref[...] = picked(skel_ref, group, low, own_ref[...], other_ref[...])


def pair(where, own, other, skel):
    return pl.pallas_call(
        pair_kernel,
        out_shape=jax.ShapeDtypeStruct(own.shape, F32),
        in_specs=[pl.BlockSpec(memory_space=pltpu.SMEM)] + [pl.BlockSpec(memory_space=pltpu.VMEM)] * 3,
        out_specs=pl.BlockSpec(memory_space=pltpu.VMEM),
        compiler_params=pltpu.CompilerParams(vmem_limit_bytes=VMEM_LIMIT),
        name="pair",
    )(where, own, other, skel)


def invert_in_place(refs):
    sub = iota((8, 128), 0)
    lane = iota((8, 128), 1)

    def along(block, index):
        return jnp.take_along_axis(block, index, axis=1)

    def step(b, carry):
        base = pl.multiple_of(b * 8, 8)
        rows = pl.ds(base, 8)
        inside = (lane >= base) & (lane < base + 8)
        indices = [jnp.full((8, 128), base + k, jnp.int32) for k in range(8)]
        for ref in refs:
            block = ref[rows, :]
            columns = [along(block, indices[k]) for k in range(8)]
            block = jnp.where(inside, jnp.where(lane - base == sub, 1.0, 0.0), block)
            for i in range(8):
                pivot = columns[i][i : i + 1, :]
                scale = 1.0 / pivot
                minus = jnp.where(sub == i, columns[i] - 1.0, columns[i])
                block = block - minus * (block[i : i + 1, :] * scale)
                for k in range(i + 1, 8):
                    columns[k] = columns[k] - minus * (columns[k][i : i + 1, :] * scale)
            for m in range(16):
                part = ref[8 * m : 8 * m + 8, :]
                total = jnp.where(inside, 0.0, part)
                for k in range(8):
                    total = total - along(part, indices[k]) * block[k : k + 1, :]
                ref[8 * m : 8 * m + 8, :] = total
            ref[rows, :] = block
        return carry

    lax.fori_loop(0, 16, step, 0)


def interp_kernel(leaf_ref, chosen_ref, pair_ref, leaf_out, merge_out, first, second):
    chosen, upper = chosen_ref[...], pair_ref[...]
    first[...] = dot(chosen, chosen, ROW_ROW, HIGHEST)
    second[...] = dot(upper, upper, ROW_ROW, HIGHEST)
    invert_in_place([first, second])
    leaf_out[...] = dot(dot(side_by_side(leaf_ref), chosen, ROW_ROW, HIGHEST), first[...], precision=HIGHEST)
    merge_out[...] = dot(dot(chosen, upper, ROW_ROW, HIGHEST), second[...], precision=HIGHEST)


def interp(leaf_rows, chosen, upper):
    return pl.pallas_call(
        interp_kernel,
        out_shape=[
            jax.ShapeDtypeStruct((leaf_rows.shape[1], RANK), F32),
            jax.ShapeDtypeStruct((RANK, RANK), F32),
        ],
        in_specs=[pl.BlockSpec(memory_space=pltpu.VMEM)] * 3,
        out_specs=[pl.BlockSpec(memory_space=pltpu.VMEM)] * 2,
        scratch_shapes=[pltpu.VMEM((RANK, RANK), F32)] * 2,
        cost_estimate=pl.CostEstimate(flops=8_000_000_000, bytes_accessed=2_000_000, transcendentals=0),
        compiler_params=pltpu.CompilerParams(vmem_limit_bytes=VMEM_LIMIT),
        name="interp",
    )(leaf_rows, chosen, upper)


def top_kernel(where_ref, own_ref, other_ref, skel_ref, top_out, rows_out, gram, quad):
    position = where_ref[0]
    group, low, high = lax.shift_right_arithmetic(position, 2), position & 1, lax.shift_right_arithmetic(position, 1) & 1
    quad[...] = picked(skel_ref, group, high, own_ref[...], other_ref[...])
    chosen = quad[...]
    gram[...] = dot(chosen, chosen, ROW_ROW, HIGHEST)
    columns = pl.ds(pl.multiple_of(where_ref[1] * 128, 128), 128)
    rows_out[...] = quad[pl.ds(pl.multiple_of((position & 3) * (RANK // 4), RANK // 4), RANK // 4), columns]
    invert_in_place([gram])
    own = own_ref[pl.ds(pl.multiple_of(low * (RANK // 2), RANK // 2), RANK // 2), :]
    top_out[...] = dot(dot(own, chosen, ROW_ROW, HIGHEST), gram[...], precision=HIGHEST)


def top(where, own, other, skel):
    return pl.pallas_call(
        top_kernel,
        out_shape=[jax.ShapeDtypeStruct((RANK // 2, RANK), F32), jax.ShapeDtypeStruct((RANK // 4, 128), F32)],
        in_specs=[pl.BlockSpec(memory_space=pltpu.SMEM)] + [pl.BlockSpec(memory_space=pltpu.VMEM)] * 3,
        out_specs=[pl.BlockSpec(memory_space=pltpu.VMEM)] * 2,
        scratch_shapes=[pltpu.VMEM((RANK, RANK), F32), pltpu.VMEM(own.shape, F32)],
        compiler_params=pltpu.CompilerParams(vmem_limit_bytes=VMEM_LIMIT),
        name="top",
    )(where, own, other, skel)


def shifted(value, axis, steps):
    count = lax.axis_size(axis)
    first, last = (max(0, -steps), min(count, count - steps))
    return lax.ppermute(value, axis, [(source, source + steps) for source in range(first, last)])


def swapped(block, axis, apart):
    count = lax.axis_size(axis)
    return lax.ppermute(block, axis, [(i, i ^ (1 << apart)) for i in range(count)])


def body(
    probe, shift_real, shift_imag, child_gen, child_coef, child_map, child_of, leaf_skel, pair_skel, quad_skel
):
    row_count, _, col_count = probe.shape
    devices = lax.axis_size("row")
    where = jnp.stack([lax.axis_index("row"), lax.axis_index("samp")]).astype(jnp.int32)
    offset = LINE // row_count
    low = shifted(probe, "row", offset)
    high = shifted(probe, "row", -offset)
    left = shifted(probe[row_count - 1 :], "row", 1)
    right = shifted(probe[:1], "row", -1)
    outgoing = route(child_map, child_of, child_gen, devices)
    flat = lambda value: value.reshape(-1, col_count)
    part = front(
        flat(probe), flat(low), flat(high), flat(left), flat(right),
        shift_real.reshape(-1, 128), shift_imag.reshape(-1, 128), flat(child_coef),
    )
    wide = lax.all_gather(part, "samp")
    got = lax.all_to_all(
        outgoing.reshape(devices * SLOT // 2, 2, -1), "row", split_axis=0, concat_axis=0, tiled=True
    ).reshape(devices * SLOT, -1)
    own, leaf_rows, chosen = leaf(where, got, wide, leaf_skel)
    upper = pair(where, chosen, swapped(chosen, "row", 0), pair_skel)
    across = swapped(upper, "row", 1)
    leaf_interp, merge_interp = interp(leaf_rows, chosen, upper)
    top_interp, top_rows = top(where, upper, across, quad_skel)
    return own.reshape(row_count, 2, col_count), leaf_interp, merge_interp, top_interp, top_rows


def solution(mesh):
    return jax.shard_map(
        body,
        mesh=mesh,
        in_specs=(
            P("row", None, "samp"),
            P("row"),
            P("row"),
            P("row", None),
            P(None, None, "samp"),
            P("row", None),
            P("row"),
            P("row", None),
            P(),
            P(),
        ),
        out_specs=(
            P("row", None, "samp"),
            P("row", None),
            P("row", None),
            P("row", None),
            P("row", "samp"),
        ),
        check_vma=False,
    )
```

```python
import functools

import jax
import jax.numpy as jnp
from jax import lax
from jax.experimental import pallas as pl
from jax.experimental.pallas import tpu as pltpu
from jax.sharding import PartitionSpec as P

LINE = 512
CAP = 8
SLOT = CAP + 2
RANK = 128
ROWS = 256
HIGHEST = lax.Precision.HIGHEST
F32 = jnp.float32
BF16 = jnp.bfloat16
VMEM_LIMIT = 24 * 1024 * 1024
VMEM_ALL = 60 * 1024 * 1024


def whole(value):
    return pl.BlockSpec(value.shape, lambda: (0,) * value.ndim)


def iota(shape, dim):
    return lax.broadcasted_iota(jnp.int32, shape, dim)


def column_of(row):
    square = jnp.broadcast_to(row, (128, 128))
    return jnp.sum(jnp.where(iota((128, 128), 0) == iota((128, 128), 1), square, jnp.zeros_like(square)), 1, keepdims=True)


def side_by_side(ref):
    return jnp.concatenate([ref[s] for s in range(ref.shape[0])], 1)


def dot(a, b, dims=(((1,), (0,)), ((), ())), precision=None):
    return lax.dot_general(a, b, dims, precision=precision, preferred_element_type=F32)


ROW_ROW = (((1,), (1,)), ((), ()))
COL_COL = (((0,), (0,)), ((), ()))


def route_kernel(of_ref, map_ref, gen_ref, out_ref):
    blocks = map_ref.shape[0]
    count = blocks * 128
    targets = map_ref[...]
    owner = lax.shift_right_arithmetic(targets, 8)
    place = (targets & (ROWS - 1)) + 1
    owner_row = jnp.concatenate([owner[b : b + 1] for b in range(blocks)], 1).astype(F32)
    owner_col = jnp.concatenate([column_of(owner[b : b + 1].astype(F32)) for b in range(blocks)], 0)
    place_col = jnp.concatenate([column_of(place[b : b + 1].astype(F32)) for b in range(blocks)], 0)
    label_col = jnp.concatenate([jnp.full((128, 1), of_ref[b], jnp.int32) for b in range(blocks)], 0).astype(F32)
    same = jnp.where(owner_col == owner_row, 1.0, 0.0)
    sub, lane = iota((count, count), 0), iota((count, count), 1)
    within_row = jnp.sum(jnp.where(sub < lane, same, 0.0), 0, keepdims=True)
    within_col = jnp.sum(jnp.where(lane < sub, same, 0.0), 1, keepdims=True)
    slot_row = jnp.where(owner_row >= 0, owner_row * SLOT + within_row, -1.0).astype(jnp.int32)
    info_row = jnp.where(owner_row >= 0, owner_row * SLOT + CAP, -1.0).astype(jnp.int32)
    lanes = iota((count, 128), 1)
    within_at = within_col.astype(jnp.int32)
    info = jnp.where(lanes == within_at, place_col, 0.0) + jnp.where(lanes == within_at + CAP, label_col, 0.0)
    table = jnp.concatenate([gen_ref[...], info.astype(BF16)], 0)
    rows = out_ref.shape[0]
    step = min(256, rows)
    for first in range(0, rows, step):
        at = iota((step, count), 0) + first
        pick = jnp.concatenate([jnp.where(at == slot_row, 1.0, 0.0), jnp.where(at == info_row, 1.0, 0.0)], 1)
        out_ref[first : first + step] = dot(pick.astype(BF16), table).astype(BF16)


def route(child_map, child_of, child_gen, devices):
    return pl.pallas_call(
        route_kernel,
        out_shape=jax.ShapeDtypeStruct((devices * SLOT, child_gen.shape[1]), BF16),
        in_specs=[pl.BlockSpec(memory_space=pltpu.SMEM), whole(child_map), whole(child_gen)],
        out_specs=pl.BlockSpec(memory_space=pltpu.VMEM),
        compiler_params=pltpu.CompilerParams(vmem_limit_bytes=VMEM_ALL),
        name="route",
    )(child_of, child_map, child_gen)


def one_hot(skel_ref, group, width, shift=0):
    picks = column_of(skel_ref[pl.ds(group, 1), :].astype(F32)).astype(jnp.int32)
    return jnp.where(iota((RANK, width), 1) == ((picks + shift) & (width - 1)), 1.0, 0.0)


def child_kernel(
    where_ref, got_ref, coef_ref, x_ref, real_ref, imag_ref, leaf_skel_ref, pair_skel_ref, quad_skel_ref,
    out_ref, leaf_pick_ref, pair_pick_ref, quad_pick_ref,
):
    position = where_ref[0]
    low, high = position & 1, lax.shift_right_arithmetic(position, 1) & 1
    leaf_pick_ref[...] = one_hot(leaf_skel_ref, 0, 2 * ROWS)
    pair_pick_ref[...] = one_hot(pair_skel_ref, lax.shift_right_arithmetic(position, 1), 2 * RANK, RANK * low)
    quad_pick_ref[...] = one_hot(quad_skel_ref, lax.shift_right_arithmetic(position, 2), 2 * RANK, RANK * high)
    rows = 2 * ROWS
    sub_x = iota((rows, 128), 0)
    half = lax.shift_right_arithmetic(iota((256, 128), 0), 1) == iota((256, 128), 1)

    def spread_rows(ref):
        blocks = [jnp.sum(jnp.where(half, ref[b : b + 1, :], 0.0), 1, keepdims=True) for b in range(ref.shape[0])]
        return jnp.concatenate(blocks, 0)

    real, imag = spread_rows(real_ref) + 4.0, spread_rows(imag_ref)
    got = got_ref[...]
    count = got.shape[0]
    sources = count // SLOT
    info_at = iota((sources, count), 0) * SLOT + CAP == iota((sources, count), 1)
    info = dot(jnp.where(info_at, 1.0, 0.0).astype(BF16), got).astype(BF16)
    along = iota((count, sources), 0)
    source = lax.shift_right_arithmetic(along * 6554, 16)
    spread = dot(jnp.where(source == iota((count, sources), 1), 1.0, 0.0).astype(BF16), info)
    sub = iota((count, 128), 0)
    slot = sub - SLOT * lax.shift_right_arithmetic(sub * 6554, 16)
    label = jnp.sum(jnp.where(iota((count, 128), 1) == slot + CAP, spread, 0.0), 1, keepdims=True)
    along_t = iota((sources, count), 1)
    source_t = lax.shift_right_arithmetic(along_t * 6554, 16)
    spread_t = dot(info, jnp.where(source_t == iota((sources, count), 0), 1.0, 0.0).astype(BF16), COL_COL)
    lane = iota((128, count), 1)
    slot_t = lane - SLOT * lax.shift_right_arithmetic(lane * 6554, 16)
    sub_t = iota((128, count), 0)
    code = jnp.sum(jnp.where((sub_t == slot_t) & (sub_t < CAP), spread_t, 0.0), 0, keepdims=True)
    onto = jnp.where(iota((ROWS, count), 0) + 1 == code.astype(jnp.int32), 1.0, 0.0).astype(BF16)
    wide = got.astype(F32)
    zero = jnp.zeros_like(wide)
    parts = jnp.concatenate([jnp.where(label == 0.0, wide, zero), jnp.where(label == 0.0, zero, wide)], 1).astype(BF16)
    rank = coef_ref.shape[1] // 2
    for s in range(coef_ref.shape[0]):
        coef = coef_ref[s]
        first, second, none = coef[:rank], coef[rank:], jnp.zeros((rank, 128), BF16)
        table = jnp.concatenate(
            [jnp.concatenate([first, none, second, none], 0), jnp.concatenate([none, first, none, second], 0)], 1
        )
        values = dot(parts, table).astype(BF16)
        sums = dot(onto, values)
        for c in range(2):
            out_ref[s, pl.ds(c, ROWS, stride=2), :] = sums[:, c * 128 : (c + 1) * 128]
        x = x_ref[s].astype(F32)
        before = jnp.where(sub_x < 2, 0.0, pltpu.roll(x, 2, 0))
        after = jnp.where(sub_x >= rows - 2, 0.0, pltpu.roll(x, rows - 2, 0))
        turned = jnp.where((sub_x & 1) == 0, -pltpu.roll(x, rows - 1, 0), pltpu.roll(x, 1, 0))
        out_ref[s] = out_ref[s] + (real * x + imag * turned - (before + after))


def child(where, got, coef, x, *others):
    return pl.pallas_call(
        child_kernel,
        out_shape=[
            jax.ShapeDtypeStruct((coef.shape[0], 2 * ROWS, coef.shape[2]), F32),
            jax.ShapeDtypeStruct((RANK, 2 * ROWS), F32),
            jax.ShapeDtypeStruct((RANK, 2 * RANK), F32),
            jax.ShapeDtypeStruct((RANK, 2 * RANK), F32),
        ],
        in_specs=[pl.BlockSpec(memory_space=pltpu.SMEM)]
        + [pl.BlockSpec(memory_space=pltpu.VMEM)] * 3
        + [whole(value) for value in others],
        out_specs=[pl.BlockSpec(memory_space=pltpu.VMEM)] * 4,
        cost_estimate=pl.CostEstimate(flops=2_000_000_000, bytes_accessed=2_000_000, transcendentals=0),
        compiler_params=pltpu.CompilerParams(vmem_limit_bytes=VMEM_LIMIT),
        name="child",
    )(where, got, coef, x, *others)


def leaf_kernel(where_ref, part_ref, low_ref, high_ref, left_ref, right_ref, pick_ref, own_ref, leaf_ref, chosen_ref):
    parts, rows, width = part_ref.shape
    sub = iota((8, width), 0)
    for s in range(parts):
        left, right = left_ref[s].astype(F32), right_ref[s].astype(F32)
        leaf_ref[s] = part_ref[s] - (low_ref[s].astype(F32) + high_ref[s].astype(F32))
        first = jnp.where(sub == 0, left[0:1], jnp.where(sub == 1, left[1:2], 0.0))
        last = jnp.where(sub == 6, right[0:1], jnp.where(sub == 7, right[1:2], 0.0))
        leaf_ref[s, 0:8, :] = leaf_ref[s, 0:8, :] - first
        leaf_ref[s, rows - 8 : rows, :] = leaf_ref[s, rows - 8 : rows, :] - last
    own_ref[...] = leaf_ref[where_ref[1]]
    chosen_ref[...] = dot(pick_ref[...], side_by_side(leaf_ref), precision=HIGHEST)


def leaf(where, part, *others):
    parts, rows, width = part.shape
    return pl.pallas_call(
        leaf_kernel,
        out_shape=[
            jax.ShapeDtypeStruct((rows, width), F32),
            jax.ShapeDtypeStruct(part.shape, F32),
            jax.ShapeDtypeStruct((RANK, parts * width), F32),
        ],
        in_specs=[pl.BlockSpec(memory_space=pltpu.SMEM)] + [pl.BlockSpec(memory_space=pltpu.VMEM)] * 6,
        out_specs=[pl.BlockSpec(memory_space=pltpu.VMEM)] * 3,
        compiler_params=pltpu.CompilerParams(vmem_limit_bytes=VMEM_LIMIT),
        name="leaf",
    )(where, part, *others)


def products_kernel(leaf_ref, chosen_ref, gram_ref, cross_ref):
    chosen = chosen_ref[...]
    gram_ref[...] = dot(chosen, chosen, ROW_ROW, HIGHEST)
    cross_ref[...] = dot(side_by_side(leaf_ref), chosen, ROW_ROW, HIGHEST)


def products(leaf_rows, chosen):
    return pl.pallas_call(
        products_kernel,
        out_shape=[
            jax.ShapeDtypeStruct((RANK, RANK), F32),
            jax.ShapeDtypeStruct((leaf_rows.shape[1], RANK), F32),
        ],
        in_specs=[pl.BlockSpec(memory_space=pltpu.VMEM)] * 2,
        out_specs=[pl.BlockSpec(memory_space=pltpu.VMEM)] * 2,
        cost_estimate=pl.CostEstimate(flops=1_000_000_000, bytes_accessed=2_000_000, transcendentals=0),
        compiler_params=pltpu.CompilerParams(vmem_limit_bytes=VMEM_LIMIT),
        name="products",
    )(leaf_rows, chosen)


def pair_kernel(pick_ref, own_ref, other_ref, out_ref):
    out_ref[...] = dot(pick_ref[...], jnp.concatenate([own_ref[...], other_ref[...]], 0), precision=HIGHEST)


def pair(pick, own, other):
    return pl.pallas_call(
        pair_kernel,
        out_shape=jax.ShapeDtypeStruct(own.shape, F32),
        in_specs=[pl.BlockSpec(memory_space=pltpu.VMEM)] * 3,
        out_specs=pl.BlockSpec(memory_space=pltpu.VMEM),
        compiler_params=pltpu.CompilerParams(vmem_limit_bytes=VMEM_LIMIT),
        name="pair",
    )(pick, own, other)


def invert_in_place(refs, width=32):
    sub = iota((8, RANK), 0)
    lane = iota((8, RANK), 1)
    wide_lane = iota((width, RANK), 1)
    count, panels = width // 8, RANK // width
    matrices = [[ref[8 * m : 8 * m + 8, :] for m in range(RANK // 8)] for ref in refs]

    def eliminated(panel, at, j):
        inside = (lane >= at) & (lane < at + 8)

        def along(block, k):
            return jnp.take_along_axis(block, jnp.full((8, RANK), at + k, jnp.int32), axis=1)

        columns = [along(panel[j], k) for k in range(8)]
        block = jnp.where(inside, jnp.where(lane - at == sub, 1.0, 0.0), panel[j])
        for i in range(8):
            minus = jnp.where(sub == i, columns[i] - 1.0, columns[i]) * (1.0 / columns[i][i : i + 1, :])
            block = block - minus * block[i : i + 1, :]
            for k in range(i + 1, 8):
                columns[k] = columns[k] - minus * columns[k][i : i + 1, :]
        result = []
        for m in range(count):
            total = block
            if m != j:
                total = jnp.where(inside, 0.0, panel[m])
                for k in range(8):
                    total = total - along(panel[m], k) * block[k : k + 1, :]
            result.append(total)
        return result

    for p in range(panels):
        base = p * width
        inside = (wide_lane >= base) & (wide_lane < base + width)
        for matrix in matrices:
            panel = matrix[p * count : (p + 1) * count]
            for j in range(count):
                panel = eliminated(panel, base + 8 * j, j)
            rows = jnp.concatenate(panel, 0)
            for q in [(p + 1 + t) % panels for t in range(panels - 1)]:
                old = jnp.concatenate(matrix[q * count : (q + 1) * count], 0)
                new = jnp.where(inside, 0.0, old) - dot(old[:, base : base + width], rows, precision=HIGHEST)
                for j in range(count):
                    matrix[q * count + j] = new[8 * j : 8 * j + 8, :]
            matrix[p * count : (p + 1) * count] = panel
    for ref, matrix in zip(refs, matrices):
        for m in range(RANK // 8):
            ref[8 * m : 8 * m + 8, :] = matrix[m]


def applied(cross, gram, inverse):
    unit = jnp.where(iota((RANK, RANK), 0) == iota((RANK, RANK), 1), 1.0, 0.0)
    rough = dot(cross, inverse, precision=HIGHEST)
    return rough + dot(rough, unit - dot(gram, inverse, precision=HIGHEST), precision=HIGHEST)


def interp_kernel(leaf_gram_ref, leaf_cross_ref, chosen_ref, upper_ref, leaf_out, merge_out, first, second):
    upper = upper_ref[...]
    merge_gram = dot(upper, upper, ROW_ROW, HIGHEST)
    first[...] = leaf_gram_ref[...]
    second[...] = merge_gram
    invert_in_place([first, second])
    merge_cross = dot(chosen_ref[...], upper, ROW_ROW, HIGHEST)
    leaf_out[...] = applied(leaf_cross_ref[...], leaf_gram_ref[...], first[...])
    merge_out[...] = applied(merge_cross, merge_gram, second[...])


def interp(leaf_gram, leaf_cross, chosen, upper):
    return pl.pallas_call(
        interp_kernel,
        out_shape=[
            jax.ShapeDtypeStruct(leaf_cross.shape, F32),
            jax.ShapeDtypeStruct((RANK, RANK), F32),
        ],
        in_specs=[pl.BlockSpec(memory_space=pltpu.VMEM)] * 4,
        out_specs=[pl.BlockSpec(memory_space=pltpu.VMEM)] * 2,
        scratch_shapes=[pltpu.VMEM((RANK, RANK), F32)] * 2,
        cost_estimate=pl.CostEstimate(flops=8_000_000_000, bytes_accessed=2_000_000, transcendentals=0),
        compiler_params=pltpu.CompilerParams(vmem_limit_bytes=VMEM_LIMIT),
        name="interp",
    )(leaf_gram, leaf_cross, chosen, upper)


def top_kernel(where_ref, pick_ref, own_ref, other_ref, top_out, rows_out, gram, quad):
    position = where_ref[0]
    chosen = dot(pick_ref[...], jnp.concatenate([own_ref[...], other_ref[...]], 0), precision=HIGHEST)
    quad[...] = chosen
    top_gram = dot(chosen, chosen, ROW_ROW, HIGHEST)
    gram[...] = top_gram
    columns = pl.ds(pl.multiple_of(where_ref[1] * 128, 128), 128)
    rows_out[...] = quad[pl.ds(pl.multiple_of((position & 3) * (RANK // 4), RANK // 4), RANK // 4), columns]
    invert_in_place([gram], 64)
    own = own_ref[pl.ds(pl.multiple_of((position & 1) * (RANK // 2), RANK // 2), RANK // 2), :]
    top_out[...] = applied(dot(own, chosen, ROW_ROW, HIGHEST), top_gram, gram[...])


def top(where, pick, own, other):
    return pl.pallas_call(
        top_kernel,
        out_shape=[jax.ShapeDtypeStruct((RANK // 2, RANK), F32), jax.ShapeDtypeStruct((RANK // 4, 128), F32)],
        in_specs=[pl.BlockSpec(memory_space=pltpu.SMEM)] + [pl.BlockSpec(memory_space=pltpu.VMEM)] * 3,
        out_specs=[pl.BlockSpec(memory_space=pltpu.VMEM)] * 2,
        scratch_shapes=[pltpu.VMEM((RANK, RANK), F32), pltpu.VMEM(own.shape, F32)],
        compiler_params=pltpu.CompilerParams(vmem_limit_bytes=VMEM_LIMIT),
        name="top",
    )(where, pick, own, other)


def shifted(value, axis, steps):
    count = lax.axis_size(axis)
    first, last = (max(0, -steps), min(count, count - steps))
    return lax.ppermute(value, axis, [(source, source + steps) for source in range(first, last)])


def swapped(block, axis, apart):
    count = lax.axis_size(axis)
    return lax.ppermute(block, axis, [(i, i ^ (1 << apart)) for i in range(count)])


def body(
    probe, shift_real, shift_imag, child_gen, child_coef, child_map, child_of, leaf_skel, pair_skel, quad_skel
):
    row_count, _, col_count = probe.shape
    devices = lax.axis_size("row")
    where = jnp.stack([lax.axis_index("row"), lax.axis_index("samp")]).astype(jnp.int32)
    offset = LINE // row_count
    everyone = lax.all_gather(
        jnp.concatenate([probe.reshape(-1, col_count), child_coef.reshape(-1, col_count)], 0), "samp"
    )
    wide, coef = everyone[:, : 2 * row_count], everyone[:, 2 * row_count :]
    outgoing = route(child_map, child_of, child_gen, devices)
    got = lax.all_to_all(
        outgoing.reshape(devices * SLOT // 2, 2, -1), "row", split_axis=0, concat_axis=0, tiled=True
    ).reshape(devices * SLOT, -1)
    low = shifted(wide, "row", offset)
    high = shifted(wide, "row", -offset)
    left = shifted(wide[:, -2:], "row", 1)
    right = shifted(wide[:, :2], "row", -1)
    part, leaf_pick, pair_pick, quad_pick = child(
        where, got, coef, wide, shift_real.reshape(-1, 128), shift_imag.reshape(-1, 128),
        leaf_skel, pair_skel, quad_skel,
    )
    own, leaf_rows, chosen = leaf(where, part, low, high, left, right, leaf_pick)
    leaf_gram, leaf_cross = products(leaf_rows, chosen)
    upper = pair(pair_pick, chosen, swapped(chosen, "row", 0))
    leaf_interp, merge_interp = interp(leaf_gram, leaf_cross, chosen, upper)
    top_interp, top_rows = top(where, quad_pick, upper, swapped(upper, "row", 1))
    return own.reshape(row_count, 2, col_count), leaf_interp, merge_interp, top_interp, top_rows


def solution(mesh):
    return jax.shard_map(
        body,
        mesh=mesh,
        in_specs=(
            P("row", None, "samp"),
            P("row"),
            P("row"),
            P("row", None),
            P(None, None, "samp"),
            P("row", None),
            P("row"),
            P("row", None),
            P(),
            P(),
        ),
        out_specs=(
            P("row", None, "samp"),
            P("row", None),
            P("row", None),
            P("row", None),
            P("row", "samp"),
        ),
        check_vma=False,
    )
```

```python
import functools

import jax
import jax.numpy as jnp
from jax import lax
from jax.experimental import pallas as pl
from jax.experimental.pallas import tpu as pltpu
from jax.sharding import PartitionSpec as P

LINE = 512
CAP = 8
SLOT = CAP + 2
RANK = 128
ROWS = 256
HIGHEST = lax.Precision.HIGHEST
F32 = jnp.float32
BF16 = jnp.bfloat16
VMEM_LIMIT = 24 * 1024 * 1024
VMEM_ALL = 60 * 1024 * 1024


def whole(value):
    return pl.BlockSpec(value.shape, lambda: (0,) * value.ndim)


def iota(shape, dim):
    return lax.broadcasted_iota(jnp.int32, shape, dim)


def column_of(row):
    square = jnp.broadcast_to(row, (128, 128))
    return jnp.sum(jnp.where(iota((128, 128), 0) == iota((128, 128), 1), square, jnp.zeros_like(square)), 1, keepdims=True)


def mask(condition):
    return jnp.where(condition, 1.0, 0.0).astype(BF16)


def picked(pick, rows):
    first = rows.astype(BF16)
    rest = rows - first.astype(F32)
    second = rest.astype(BF16)
    third = (rest - second.astype(F32)).astype(BF16)
    return dot(pick, first) + dot(pick, second) + dot(pick, third)


def side_by_side(ref):
    return jnp.concatenate([ref[s] for s in range(ref.shape[0])], 1)


def dot(a, b, dims=(((1,), (0,)), ((), ())), precision=None):
    return lax.dot_general(a, b, dims, precision=precision, preferred_element_type=F32)


ROW_ROW = (((1,), (1,)), ((), ()))
COL_COL = (((0,), (0,)), ((), ()))


def route_kernel(of_ref, map_ref, gen_ref, out_ref):
    blocks = map_ref.shape[0]
    count = blocks * 128
    targets = map_ref[...]
    owner = lax.shift_right_arithmetic(targets, 8)
    place = (targets & (ROWS - 1)) + 1
    owner_row = jnp.concatenate([owner[b : b + 1] for b in range(blocks)], 1).astype(F32)
    owner_col = jnp.concatenate([column_of(owner[b : b + 1].astype(F32)) for b in range(blocks)], 0)
    place_col = jnp.concatenate([column_of(place[b : b + 1].astype(F32)) for b in range(blocks)], 0)
    label_col = jnp.concatenate([jnp.full((128, 1), of_ref[b], jnp.int32) for b in range(blocks)], 0).astype(F32)
    same = jnp.where(owner_col == owner_row, 1.0, 0.0)
    sub, lane = iota((count, count), 0), iota((count, count), 1)
    within_row = jnp.sum(jnp.where(sub < lane, same, 0.0), 0, keepdims=True)
    within_col = jnp.sum(jnp.where(lane < sub, same, 0.0), 1, keepdims=True)
    slot_row = jnp.where(owner_row >= 0, owner_row * SLOT + within_row, -1.0).astype(jnp.int32)
    lanes = iota((count, 128), 1)
    within_at = within_col.astype(jnp.int32)
    info = jnp.where(lanes == within_at, place_col, 0.0) + jnp.where(lanes == within_at + CAP, label_col, 0.0)
    owns = mask(iota((RANK, count), 0) == owner_row.astype(jnp.int32))
    table = jnp.concatenate([gen_ref[...], dot(owns, info.astype(BF16)).astype(BF16)], 0)
    rows = out_ref.shape[0]
    info_row = iota((1, RANK), 1) * SLOT + CAP
    source_row = jnp.concatenate([slot_row, info_row], 1)
    step = min(256, rows)
    for first in range(0, rows, step):
        pick = mask(iota((step, count + RANK), 0) + first == source_row)
        out_ref[first : first + step] = dot(pick, table).astype(BF16)


def route(child_map, child_of, child_gen, devices):
    return pl.pallas_call(
        route_kernel,
        out_shape=jax.ShapeDtypeStruct((devices * SLOT, child_gen.shape[1]), BF16),
        in_specs=[pl.BlockSpec(memory_space=pltpu.SMEM), whole(child_map), whole(child_gen)],
        out_specs=pl.BlockSpec(memory_space=pltpu.VMEM),
        compiler_params=pltpu.CompilerParams(vmem_limit_bytes=VMEM_ALL),
        name="route",
    )(child_of, child_map, child_gen)


def one_hot(skel_ref, group, width, shift=0):
    picks = column_of(skel_ref[pl.ds(group, 1), :].astype(F32)).astype(jnp.int32)
    return mask(iota((RANK, width), 1) == ((picks + shift) & (width - 1)))


def child_kernel(
    where_ref, got_ref, coef_ref, x_ref, real_ref, imag_ref, leaf_skel_ref, pair_skel_ref, quad_skel_ref,
    out_ref, leaf_pick_ref, pair_pick_ref, quad_pick_ref,
):
    position = where_ref[0]
    low, high = position & 1, lax.shift_right_arithmetic(position, 1) & 1
    leaf_pick_ref[...] = one_hot(leaf_skel_ref, 0, 2 * ROWS)
    pair_pick_ref[...] = one_hot(pair_skel_ref, lax.shift_right_arithmetic(position, 1), 2 * RANK, RANK * low)
    quad_pick_ref[...] = one_hot(quad_skel_ref, lax.shift_right_arithmetic(position, 2), 2 * RANK, RANK * high)
    rows = 2 * ROWS
    sub_x = iota((rows, 128), 0)
    half = lax.shift_right_arithmetic(iota((256, 128), 0), 1) == iota((256, 128), 1)

    def spread_rows(ref):
        blocks = [jnp.sum(jnp.where(half, ref[b : b + 1, :], 0.0), 1, keepdims=True) for b in range(ref.shape[0])]
        return jnp.concatenate(blocks, 0)

    real, imag = spread_rows(real_ref) + 4.0, spread_rows(imag_ref)
    got = got_ref[...]
    count = got.shape[0]
    sources = count // SLOT
    info_at = iota((sources, count), 0) * SLOT + CAP == iota((sources, count), 1)
    info = dot(jnp.where(info_at, 1.0, 0.0).astype(BF16), got).astype(BF16)
    along = iota((count, sources), 0)
    source = lax.shift_right_arithmetic(along * 6554, 16)
    spread = dot(jnp.where(source == iota((count, sources), 1), 1.0, 0.0).astype(BF16), info)
    sub = iota((count, 128), 0)
    slot = sub - SLOT * lax.shift_right_arithmetic(sub * 6554, 16)
    ones = jnp.full((128, 128), 1.0, BF16)
    label = dot(jnp.where(iota((count, 128), 1) == slot + CAP, spread, 0.0).astype(BF16), ones)
    along_t = iota((sources, count), 1)
    source_t = lax.shift_right_arithmetic(along_t * 6554, 16)
    spread_t = dot(info, jnp.where(source_t == iota((sources, count), 0), 1.0, 0.0).astype(BF16), COL_COL)
    lane = iota((128, count), 1)
    slot_t = lane - SLOT * lax.shift_right_arithmetic(lane * 6554, 16)
    sub_t = iota((128, count), 0)
    code = jnp.sum(jnp.where((sub_t == slot_t) & (sub_t < CAP), spread_t, 0.0), 0, keepdims=True)
    onto = jnp.where(iota((ROWS, count), 0) + 1 == code.astype(jnp.int32), 1.0, 0.0).astype(BF16)
    second = got * label.astype(BF16)
    parts = jnp.concatenate([got - second, second], 1)
    rank = coef_ref.shape[1] // 2
    for s in range(coef_ref.shape[0]):
        coef = coef_ref[s]
        first, second, none = coef[:rank], coef[rank:], jnp.zeros((rank, 128), BF16)
        table = jnp.concatenate(
            [jnp.concatenate([first, none, second, none], 0), jnp.concatenate([none, first, none, second], 0)], 1
        )
        values = dot(parts, table).astype(BF16)
        sums = dot(onto, values)
        for c in range(2):
            out_ref[s, pl.ds(c, ROWS, stride=2), :] = sums[:, c * 128 : (c + 1) * 128]
        x = x_ref[s].astype(F32)
        before = jnp.where(sub_x < 2, 0.0, pltpu.roll(x, 2, 0))
        after = jnp.where(sub_x >= rows - 2, 0.0, pltpu.roll(x, rows - 2, 0))
        turned = jnp.where((sub_x & 1) == 0, -pltpu.roll(x, rows - 1, 0), pltpu.roll(x, 1, 0))
        out_ref[s] = out_ref[s] + (real * x + imag * turned - (before + after))


def child(where, got, coef, x, *others):
    return pl.pallas_call(
        child_kernel,
        out_shape=[
            jax.ShapeDtypeStruct((coef.shape[0], 2 * ROWS, coef.shape[2]), F32),
            jax.ShapeDtypeStruct((RANK, 2 * ROWS), BF16),
            jax.ShapeDtypeStruct((RANK, 2 * RANK), BF16),
            jax.ShapeDtypeStruct((RANK, 2 * RANK), BF16),
        ],
        in_specs=[pl.BlockSpec(memory_space=pltpu.SMEM)]
        + [pl.BlockSpec(memory_space=pltpu.VMEM)] * 3
        + [whole(value) for value in others],
        out_specs=[pl.BlockSpec(memory_space=pltpu.VMEM)] * 4,
        cost_estimate=pl.CostEstimate(flops=2_000_000_000, bytes_accessed=2_000_000, transcendentals=0),
        compiler_params=pltpu.CompilerParams(vmem_limit_bytes=VMEM_LIMIT),
        name="child",
    )(where, got, coef, x, *others)


def leaf_kernel(where_ref, part_ref, low_ref, high_ref, left_ref, right_ref, pick_ref, own_ref, leaf_ref, chosen_ref):
    parts, rows, width = part_ref.shape
    sub = iota((8, width), 0)
    for s in range(parts):
        left, right = left_ref[s].astype(F32), right_ref[s].astype(F32)
        leaf_ref[s] = part_ref[s] - (low_ref[s].astype(F32) + high_ref[s].astype(F32))
        first = jnp.where(sub == 0, left[0:1], jnp.where(sub == 1, left[1:2], 0.0))
        last = jnp.where(sub == 6, right[0:1], jnp.where(sub == 7, right[1:2], 0.0))
        leaf_ref[s, 0:8, :] = leaf_ref[s, 0:8, :] - first
        leaf_ref[s, rows - 8 : rows, :] = leaf_ref[s, rows - 8 : rows, :] - last
    own_ref[...] = leaf_ref[where_ref[1]]
    chosen_ref[...] = picked(pick_ref[...], side_by_side(leaf_ref))


def leaf(where, part, *others):
    parts, rows, width = part.shape
    return pl.pallas_call(
        leaf_kernel,
        out_shape=[
            jax.ShapeDtypeStruct((rows, width), F32),
            jax.ShapeDtypeStruct(part.shape, F32),
            jax.ShapeDtypeStruct((RANK, parts * width), F32),
        ],
        in_specs=[pl.BlockSpec(memory_space=pltpu.SMEM)] + [pl.BlockSpec(memory_space=pltpu.VMEM)] * 6,
        out_specs=[pl.BlockSpec(memory_space=pltpu.VMEM)] * 3,
        compiler_params=pltpu.CompilerParams(vmem_limit_bytes=VMEM_LIMIT),
        name="leaf",
    )(where, part, *others)


def products_kernel(leaf_ref, chosen_ref, gram_ref, cross_ref):
    chosen = chosen_ref[...]
    gram_ref[...] = dot(chosen, chosen, ROW_ROW, HIGHEST)
    cross_ref[...] = dot(side_by_side(leaf_ref), chosen, ROW_ROW, HIGHEST)


def products(leaf_rows, chosen):
    return pl.pallas_call(
        products_kernel,
        out_shape=[
            jax.ShapeDtypeStruct((RANK, RANK), F32),
            jax.ShapeDtypeStruct((leaf_rows.shape[1], RANK), F32),
        ],
        in_specs=[pl.BlockSpec(memory_space=pltpu.VMEM)] * 2,
        out_specs=[pl.BlockSpec(memory_space=pltpu.VMEM)] * 2,
        cost_estimate=pl.CostEstimate(flops=1_000_000_000, bytes_accessed=2_000_000, transcendentals=0),
        compiler_params=pltpu.CompilerParams(vmem_limit_bytes=VMEM_LIMIT),
        name="products",
    )(leaf_rows, chosen)


def pair_kernel(pick_ref, own_ref, other_ref, out_ref):
    out_ref[...] = picked(pick_ref[...], jnp.concatenate([own_ref[...], other_ref[...]], 0))


def pair(pick, own, other):
    return pl.pallas_call(
        pair_kernel,
        out_shape=jax.ShapeDtypeStruct(own.shape, F32),
        in_specs=[pl.BlockSpec(memory_space=pltpu.VMEM)] * 3,
        out_specs=pl.BlockSpec(memory_space=pltpu.VMEM),
        compiler_params=pltpu.CompilerParams(vmem_limit_bytes=VMEM_LIMIT),
        name="pair",
    )(pick, own, other)


def total(terms):
    while len(terms) > 1:
        terms = [terms[i] + terms[i + 1] for i in range(0, len(terms), 2)]
    return terms[0]


def eliminated(panel, at, j):
    sub = iota((8, RANK), 0)
    lane = iota((8, RANK), 1)
    inside = (lane >= at) & (lane < at + 8)

    def along(block, k):
        return jnp.take_along_axis(block, jnp.full((8, RANK), at + k, jnp.int32), axis=1)

    columns = [along(panel[j], k) for k in range(8)]
    block = jnp.where(inside, jnp.where(lane - at == sub, 1.0, 0.0), panel[j])
    for i in range(8):
        here = sub == i
        scale = 1.0 / columns[i][i : i + 1, :]
        factor = jnp.where(here, scale, -columns[i] * scale)

        def reduced(value):
            return jnp.where(here, 0.0, value) + factor * value[i : i + 1, :]

        block = reduced(block)
        columns = columns[: i + 1] + [reduced(column) for column in columns[i + 1 :]]
    return [
        block
        if m == j
        else jnp.where(inside, 0.0, panel[m]) - total([along(panel[m], k) * block[k : k + 1, :] for k in range(8)])
        for m in range(len(panel))
    ]


def inverses(grams, width):
    wide_lane = iota((width, RANK), 1)
    count, panels = width // 8, RANK // width
    matrices = [[gram[8 * m : 8 * m + 8, :] for m in range(RANK // 8)] for gram in grams]
    for p in range(panels):
        base = p * width
        inside = (wide_lane >= base) & (wide_lane < base + width)
        for matrix in matrices:
            panel = matrix[p * count : (p + 1) * count]
            for j in range(count):
                panel = eliminated(panel, base + 8 * j, j)
            rows = jnp.concatenate(panel, 0)
            for q in [(p + 1 + t) % panels for t in range(panels - 1)]:
                old = jnp.concatenate(matrix[q * count : (q + 1) * count], 0)
                new = jnp.where(inside, 0.0, old) - dot(old[:, base : base + width], rows, precision=HIGHEST)
                matrix[q * count : (q + 1) * count] = [new[8 * j : 8 * j + 8, :] for j in range(count)]
            matrix[p * count : (p + 1) * count] = panel
    return [jnp.concatenate(matrix, 0) for matrix in matrices]


def invert_between(ref, first, last, width):
    lane = iota((RANK, RANK), 1)
    count = width // 8

    def step(p, carry):
        base = pl.multiple_of(p * width, width)
        panel = [ref[pl.ds(base + 8 * j, 8), :] for j in range(count)]
        for j in range(count):
            panel = eliminated(panel, base + 8 * j, j)
        whole_matrix = ref[...]
        left = pltpu.roll(whole_matrix, RANK - base, 1)[:, :width]
        kept = jnp.where((lane >= base) & (lane < base + width), 0.0, whole_matrix)
        ref[...] = kept - dot(left, jnp.concatenate(panel, 0), precision=HIGHEST)
        for j in range(count):
            ref[pl.ds(base + 8 * j, 8), :] = panel[j]
        return carry

    lax.fori_loop(first, last, step, 0)


def half_rows(where_ref, upper_ref):
    half = RANK // 2
    return upper_ref[pl.ds(pl.multiple_of((where_ref[0] & 1) * half, half), half), :]


def interp_kernel(
    where_ref, leaf_gram_ref, leaf_cross_ref, chosen_ref, upper_ref, pick_ref,
    leaf_out, merge_out, mine_out, inverse_out, part_out, count_out,
):
    upper = upper_ref[...]
    pick = pick_ref[:, :RANK]
    mine = picked(pick, upper)
    mine_out[...] = mine
    taken = jnp.sum(pick.astype(F32), 1, keepdims=True)
    count_out[0] = jnp.sum(taken).astype(jnp.int32)
    diagonal = iota((RANK, RANK), 0) == iota((RANK, RANK), 1)
    others = jnp.where(diagonal, 1.0 - taken, 0.0)
    leaf_inverse, merge_inverse, mine_inverse = inverses(
        [leaf_gram_ref[...], dot(upper, upper, ROW_ROW, HIGHEST), dot(mine, mine, ROW_ROW, HIGHEST) + others], 32
    )
    inverse_out[...] = mine_inverse - others
    merge_cross = dot(chosen_ref[...], upper, ROW_ROW, HIGHEST)
    half = half_rows(where_ref, upper_ref)
    part_out[...] = dot(dot(half, mine, ROW_ROW, HIGHEST), mine_inverse - others, precision=HIGHEST)
    leaf_out[...] = dot(leaf_cross_ref[...], leaf_inverse, precision=HIGHEST)
    merge_out[...] = dot(merge_cross, merge_inverse, precision=HIGHEST)


def interp(where, leaf_gram, leaf_cross, chosen, upper, pick):
    return pl.pallas_call(
        interp_kernel,
        out_shape=[
            jax.ShapeDtypeStruct(leaf_cross.shape, F32),
            jax.ShapeDtypeStruct((RANK, RANK), F32),
            jax.ShapeDtypeStruct(upper.shape, F32),
            jax.ShapeDtypeStruct((RANK, RANK), F32),
            jax.ShapeDtypeStruct((RANK // 2, RANK), F32),
            jax.ShapeDtypeStruct((1,), jnp.int32),
        ],
        in_specs=[pl.BlockSpec(memory_space=pltpu.SMEM)] + [pl.BlockSpec(memory_space=pltpu.VMEM)] * 5,
        out_specs=[pl.BlockSpec(memory_space=pltpu.VMEM)] * 5 + [pl.BlockSpec(memory_space=pltpu.SMEM)],
        cost_estimate=pl.CostEstimate(flops=8_000_000_000, bytes_accessed=2_000_000, transcendentals=0),
        compiler_params=pltpu.CompilerParams(vmem_limit_bytes=VMEM_LIMIT),
        name="interp",
    )(where, leaf_gram, leaf_cross, chosen, upper, pick)


def top_kernel(
    where_ref, count_ref, pick_ref, upper_ref, across_ref, mine_ref, inverse_ref, part_ref,
    top_out, rows_out, rest, quad,
):
    position, width = where_ref[0], 16
    pick = pick_ref[:, RANK:]
    theirs = picked(pick, across_ref[...])
    mine, inverse, part = mine_ref[...], inverse_ref[...], part_ref[...]
    quad[...] = mine + theirs
    columns = pl.ds(pl.multiple_of(where_ref[1] * 128, 128), 128)
    rows_out[...] = quad[pl.ds(pl.multiple_of((position & 3) * (RANK // 4), RANK // 4), RANK // 4), columns]
    mixed = dot(mine, theirs, ROW_ROW, HIGHEST)
    passed = dot(inverse, mixed, precision=HIGHEST)
    taken = jnp.sum(pick.astype(F32), 1, keepdims=True)
    diagonal = iota((RANK, RANK), 0) == iota((RANK, RANK), 1)
    rest[...] = (
        dot(theirs, theirs, ROW_ROW, HIGHEST)
        - dot(mixed, passed, COL_COL, HIGHEST)
        + jnp.where(diagonal, 1.0 - taken, 0.0)
    )
    half = half_rows(where_ref, upper_ref)
    cross = dot(half, theirs, ROW_ROW, HIGHEST) - dot(part, mixed, precision=HIGHEST)
    own_count = count_ref[0]
    own_first = (lax.shift_right_arithmetic(position, 1) & 1) == 0
    begin = jnp.where(own_first, own_count, 0)
    end = jnp.where(own_first, RANK, RANK - own_count)
    invert_between(
        rest, lax.shift_right_arithmetic(begin, 4), lax.shift_right_arithmetic(end + width - 1, 4), width
    )
    side = dot(cross, rest[...], precision=HIGHEST)
    top_out[...] = part + side - dot(side, passed, ROW_ROW, HIGHEST)


def top(where, count, pick, upper, across, mine, inverse, part):
    return pl.pallas_call(
        top_kernel,
        out_shape=[jax.ShapeDtypeStruct((RANK // 2, RANK), F32), jax.ShapeDtypeStruct((RANK // 4, 128), F32)],
        in_specs=[pl.BlockSpec(memory_space=pltpu.SMEM)] * 2 + [pl.BlockSpec(memory_space=pltpu.VMEM)] * 6,
        out_specs=[pl.BlockSpec(memory_space=pltpu.VMEM)] * 2,
        scratch_shapes=[pltpu.VMEM((RANK, RANK), F32), pltpu.VMEM(upper.shape, F32)],
        compiler_params=pltpu.CompilerParams(vmem_limit_bytes=VMEM_LIMIT),
        name="top",
    )(where, count, pick, upper, across, mine, inverse, part)


def shifted(value, axis, steps):
    count = lax.axis_size(axis)
    first, last = (max(0, -steps), min(count, count - steps))
    return lax.ppermute(value, axis, [(source, source + steps) for source in range(first, last)])


def swapped(block, axis, apart):
    count = lax.axis_size(axis)
    return lax.ppermute(block, axis, [(i, i ^ (1 << apart)) for i in range(count)])


def body(
    probe, shift_real, shift_imag, child_gen, child_coef, child_map, child_of, leaf_skel, pair_skel, quad_skel
):
    row_count, _, col_count = probe.shape
    devices = lax.axis_size("row")
    where = jnp.stack([lax.axis_index("row"), lax.axis_index("samp")]).astype(jnp.int32)
    offset = LINE // row_count
    everyone = lax.all_gather(
        jnp.concatenate([probe.reshape(-1, col_count), child_coef.reshape(-1, col_count)], 0), "samp"
    )
    wide, coef = everyone[:, : 2 * row_count], everyone[:, 2 * row_count :]
    outgoing = route(child_map, child_of, child_gen, devices)
    got = lax.all_to_all(
        outgoing.reshape(devices * SLOT // 2, 2, -1), "row", split_axis=0, concat_axis=0, tiled=True
    ).reshape(devices * SLOT, -1)
    low = shifted(wide, "row", offset)
    high = shifted(wide, "row", -offset)
    left = shifted(wide[:, -2:], "row", 1)
    right = shifted(wide[:, :2], "row", -1)
    base, leaf_pick, pair_pick, quad_pick = child(
        where, got, coef, wide, shift_real.reshape(-1, 128), shift_imag.reshape(-1, 128),
        leaf_skel, pair_skel, quad_skel,
    )
    own, leaf_rows, chosen = leaf(where, base, low, high, left, right, leaf_pick)
    leaf_gram, leaf_cross = products(leaf_rows, chosen)
    upper = pair(pair_pick, chosen, swapped(chosen, "row", 0))
    leaf_interp, merge_interp, mine, inverse, part, count = interp(
        where, leaf_gram, leaf_cross, chosen, upper, quad_pick
    )
    top_interp, top_rows = top(where, count, quad_pick, upper, swapped(upper, "row", 1), mine, inverse, part)
    return own.reshape(row_count, 2, col_count), leaf_interp, merge_interp, top_interp, top_rows


def solution(mesh):
    return jax.shard_map(
        body,
        mesh=mesh,
        in_specs=(
            P("row", None, "samp"),
            P("row"),
            P("row"),
            P("row", None),
            P(None, None, "samp"),
            P("row", None),
            P("row"),
            P("row", None),
            P(),
            P(),
        ),
        out_specs=(
            P("row", None, "samp"),
            P("row", None),
            P("row", None),
            P("row", None),
            P("row", "samp"),
        ),
        check_vma=False,
    )
```

```python
import functools

import jax
import jax.numpy as jnp
from jax import lax
from jax.experimental import pallas as pl
from jax.experimental.pallas import tpu as pltpu
from jax.sharding import PartitionSpec as P

LINE = 512
CAP = 8
SLOT = CAP + 2
RANK = 128
ROWS = 256
HIGHEST = lax.Precision.HIGHEST
F32 = jnp.float32
BF16 = jnp.bfloat16
VMEM_LIMIT = 24 * 1024 * 1024
VMEM_ALL = 60 * 1024 * 1024


def whole(value):
    return pl.BlockSpec(value.shape, lambda: (0,) * value.ndim)


def iota(shape, dim):
    return lax.broadcasted_iota(jnp.int32, shape, dim)


def column_of(row):
    square = jnp.broadcast_to(row, (128, 128))
    return jnp.sum(jnp.where(iota((128, 128), 0) == iota((128, 128), 1), square, jnp.zeros_like(square)), 1, keepdims=True)


def mask(condition):
    return jnp.where(condition, 1.0, 0.0).astype(BF16)


def picked(pick, rows):
    first = rows.astype(BF16)
    rest = rows - first.astype(F32)
    second = rest.astype(BF16)
    third = (rest - second.astype(F32)).astype(BF16)
    return dot(pick, first) + dot(pick, second) + dot(pick, third)


def side_by_side(ref):
    return jnp.concatenate([ref[s] for s in range(ref.shape[0])], 1)


def dot(a, b, dims=(((1,), (0,)), ((), ())), precision=None):
    return lax.dot_general(a, b, dims, precision=precision, preferred_element_type=F32)


ROW_ROW = (((1,), (1,)), ((), ()))
COL_COL = (((0,), (0,)), ((), ()))


def route_kernel(of_ref, map_ref, gen_ref, out_ref):
    blocks = map_ref.shape[0]
    count = blocks * 128
    targets = map_ref[...]
    owner = lax.shift_right_arithmetic(targets, 8)
    place = (targets & (ROWS - 1)) + 1
    owner_row = jnp.concatenate([owner[b : b + 1] for b in range(blocks)], 1).astype(F32)
    owner_col = jnp.concatenate([column_of(owner[b : b + 1].astype(F32)) for b in range(blocks)], 0)
    place_col = jnp.concatenate([column_of(place[b : b + 1].astype(F32)) for b in range(blocks)], 0)
    label_col = jnp.concatenate([jnp.full((128, 1), of_ref[b], jnp.int32) for b in range(blocks)], 0).astype(F32)
    same = jnp.where(owner_col == owner_row, 1.0, 0.0)
    sub, lane = iota((count, count), 0), iota((count, count), 1)
    within_row = jnp.sum(jnp.where(sub < lane, same, 0.0), 0, keepdims=True)
    within_col = jnp.sum(jnp.where(lane < sub, same, 0.0), 1, keepdims=True)
    slot_row = jnp.where(owner_row >= 0, owner_row * SLOT + within_row, -1.0).astype(jnp.int32)
    lanes = iota((count, 128), 1)
    within_at = within_col.astype(jnp.int32)
    info = jnp.where(lanes == within_at, place_col, 0.0) + jnp.where(lanes == within_at + CAP, label_col, 0.0)
    owns = mask(iota((RANK, count), 0) == owner_row.astype(jnp.int32))
    table = jnp.concatenate([gen_ref[...], dot(owns, info.astype(BF16)).astype(BF16)], 0)
    rows = out_ref.shape[0]
    info_row = iota((1, RANK), 1) * SLOT + CAP
    source_row = jnp.concatenate([slot_row, info_row], 1)
    step = min(256, rows)
    for first in range(0, rows, step):
        pick = mask(iota((step, count + RANK), 0) + first == source_row)
        out_ref[first : first + step] = dot(pick, table).astype(BF16)


def route(child_map, child_of, child_gen, devices):
    return pl.pallas_call(
        route_kernel,
        out_shape=jax.ShapeDtypeStruct((devices * SLOT, child_gen.shape[1]), BF16),
        in_specs=[pl.BlockSpec(memory_space=pltpu.SMEM), whole(child_map), whole(child_gen)],
        out_specs=pl.BlockSpec(memory_space=pltpu.VMEM),
        compiler_params=pltpu.CompilerParams(vmem_limit_bytes=VMEM_ALL),
        name="route",
    )(child_of, child_map, child_gen)


def one_hot(skel_ref, group, width, shift=0):
    picks = column_of(skel_ref[pl.ds(group, 1), :].astype(F32)).astype(jnp.int32)
    return mask(iota((RANK, width), 1) == ((picks + shift) & (width - 1)))


def child_kernel(
    where_ref, got_ref, coef_ref, x_ref, real_ref, imag_ref, leaf_skel_ref, pair_skel_ref, quad_skel_ref,
    out_ref, leaf_pick_ref, pair_pick_ref, quad_pick_ref,
):
    position = where_ref[0]
    low, high = position & 1, lax.shift_right_arithmetic(position, 1) & 1
    leaf_pick_ref[...] = one_hot(leaf_skel_ref, 0, 2 * ROWS)
    pair_pick_ref[...] = one_hot(pair_skel_ref, lax.shift_right_arithmetic(position, 1), 2 * RANK, RANK * low)
    quad_pick_ref[...] = one_hot(quad_skel_ref, lax.shift_right_arithmetic(position, 2), 2 * RANK, RANK * high)
    rows = 2 * ROWS
    sub_x = iota((rows, 128), 0)
    half = lax.shift_right_arithmetic(iota((256, 128), 0), 1) == iota((256, 128), 1)

    def spread_rows(ref):
        blocks = [jnp.sum(jnp.where(half, ref[b : b + 1, :], 0.0), 1, keepdims=True) for b in range(ref.shape[0])]
        return jnp.concatenate(blocks, 0)

    real, imag = spread_rows(real_ref) + 4.0, spread_rows(imag_ref)
    got = got_ref[...]
    count = got.shape[0]
    sources = count // SLOT
    info_at = iota((sources, count), 0) * SLOT + CAP == iota((sources, count), 1)
    info = dot(jnp.where(info_at, 1.0, 0.0).astype(BF16), got).astype(BF16)
    along = iota((count, sources), 0)
    source = lax.shift_right_arithmetic(along * 6554, 16)
    spread = dot(jnp.where(source == iota((count, sources), 1), 1.0, 0.0).astype(BF16), info)
    sub = iota((count, 128), 0)
    slot = sub - SLOT * lax.shift_right_arithmetic(sub * 6554, 16)
    ones = jnp.full((128, 128), 1.0, BF16)
    label = dot(jnp.where(iota((count, 128), 1) == slot + CAP, spread, 0.0).astype(BF16), ones)
    along_t = iota((sources, count), 1)
    source_t = lax.shift_right_arithmetic(along_t * 6554, 16)
    spread_t = dot(info, jnp.where(source_t == iota((sources, count), 0), 1.0, 0.0).astype(BF16), COL_COL)
    lane = iota((128, count), 1)
    slot_t = lane - SLOT * lax.shift_right_arithmetic(lane * 6554, 16)
    sub_t = iota((128, count), 0)
    code = jnp.sum(jnp.where((sub_t == slot_t) & (sub_t < CAP), spread_t, 0.0), 0, keepdims=True)
    onto = jnp.where(iota((ROWS, count), 0) + 1 == code.astype(jnp.int32), 1.0, 0.0).astype(BF16)
    second = got * label.astype(BF16)
    parts = jnp.concatenate([got - second, second], 1)
    rank = coef_ref.shape[1] // 2
    for s in range(coef_ref.shape[0]):
        coef = coef_ref[s]
        first, second, none = coef[:rank], coef[rank:], jnp.zeros((rank, 128), BF16)
        table = jnp.concatenate(
            [jnp.concatenate([first, none, second, none], 0), jnp.concatenate([none, first, none, second], 0)], 1
        )
        values = dot(parts, table).astype(BF16)
        sums = dot(onto, values)
        for c in range(2):
            out_ref[s, pl.ds(c, ROWS, stride=2), :] = sums[:, c * 128 : (c + 1) * 128]
        x = x_ref[s].astype(F32)
        before = jnp.where(sub_x < 2, 0.0, pltpu.roll(x, 2, 0))
        after = jnp.where(sub_x >= rows - 2, 0.0, pltpu.roll(x, rows - 2, 0))
        turned = jnp.where((sub_x & 1) == 0, -pltpu.roll(x, rows - 1, 0), pltpu.roll(x, 1, 0))
        out_ref[s] = out_ref[s] + (real * x + imag * turned - (before + after))


def child(where, got, coef, x, *others):
    return pl.pallas_call(
        child_kernel,
        out_shape=[
            jax.ShapeDtypeStruct((coef.shape[0], 2 * ROWS, coef.shape[2]), F32),
            jax.ShapeDtypeStruct((RANK, 2 * ROWS), BF16),
            jax.ShapeDtypeStruct((RANK, 2 * RANK), BF16),
            jax.ShapeDtypeStruct((RANK, 2 * RANK), BF16),
        ],
        in_specs=[pl.BlockSpec(memory_space=pltpu.SMEM)]
        + [pl.BlockSpec(memory_space=pltpu.VMEM)] * 3
        + [whole(value) for value in others],
        out_specs=[pl.BlockSpec(memory_space=pltpu.VMEM)] * 4,
        cost_estimate=pl.CostEstimate(flops=2_000_000_000, bytes_accessed=2_000_000, transcendentals=0),
        compiler_params=pltpu.CompilerParams(vmem_limit_bytes=VMEM_LIMIT),
        name="child",
    )(where, got, coef, x, *others)


def leaf_kernel(where_ref, part_ref, low_ref, high_ref, left_ref, right_ref, pick_ref, own_ref, leaf_ref, chosen_ref):
    parts, rows, width = part_ref.shape
    sub = iota((8, width), 0)
    for s in range(parts):
        left, right = left_ref[s].astype(F32), right_ref[s].astype(F32)
        leaf_ref[s] = part_ref[s] - (low_ref[s].astype(F32) + high_ref[s].astype(F32))
        first = jnp.where(sub == 0, left[0:1], jnp.where(sub == 1, left[1:2], 0.0))
        last = jnp.where(sub == 6, right[0:1], jnp.where(sub == 7, right[1:2], 0.0))
        leaf_ref[s, 0:8, :] = leaf_ref[s, 0:8, :] - first
        leaf_ref[s, rows - 8 : rows, :] = leaf_ref[s, rows - 8 : rows, :] - last
    own_ref[...] = leaf_ref[where_ref[1]]
    chosen_ref[...] = picked(pick_ref[...], side_by_side(leaf_ref))


def leaf(where, part, *others):
    parts, rows, width = part.shape
    return pl.pallas_call(
        leaf_kernel,
        out_shape=[
            jax.ShapeDtypeStruct((rows, width), F32),
            jax.ShapeDtypeStruct(part.shape, F32),
            jax.ShapeDtypeStruct((RANK, parts * width), F32),
        ],
        in_specs=[pl.BlockSpec(memory_space=pltpu.SMEM)] + [pl.BlockSpec(memory_space=pltpu.VMEM)] * 6,
        out_specs=[pl.BlockSpec(memory_space=pltpu.VMEM)] * 3,
        compiler_params=pltpu.CompilerParams(vmem_limit_bytes=VMEM_LIMIT),
        name="leaf",
    )(where, part, *others)


def products_kernel(leaf_ref, chosen_ref, gram_ref, cross_ref):
    chosen = chosen_ref[...]
    gram_ref[...] = dot(chosen, chosen, ROW_ROW, HIGHEST)
    cross_ref[...] = dot(side_by_side(leaf_ref), chosen, ROW_ROW, HIGHEST)


def products(leaf_rows, chosen):
    return pl.pallas_call(
        products_kernel,
        out_shape=[
            jax.ShapeDtypeStruct((RANK, RANK), F32),
            jax.ShapeDtypeStruct((leaf_rows.shape[1], RANK), F32),
        ],
        in_specs=[pl.BlockSpec(memory_space=pltpu.VMEM)] * 2,
        out_specs=[pl.BlockSpec(memory_space=pltpu.VMEM)] * 2,
        cost_estimate=pl.CostEstimate(flops=1_000_000_000, bytes_accessed=2_000_000, transcendentals=0),
        compiler_params=pltpu.CompilerParams(vmem_limit_bytes=VMEM_LIMIT),
        name="products",
    )(leaf_rows, chosen)


def pair_kernel(pick_ref, own_ref, other_ref, out_ref):
    out_ref[...] = picked(pick_ref[...], jnp.concatenate([own_ref[...], other_ref[...]], 0))


def pair(pick, own, other):
    return pl.pallas_call(
        pair_kernel,
        out_shape=jax.ShapeDtypeStruct(own.shape, F32),
        in_specs=[pl.BlockSpec(memory_space=pltpu.VMEM)] * 3,
        out_specs=pl.BlockSpec(memory_space=pltpu.VMEM),
        compiler_params=pltpu.CompilerParams(vmem_limit_bytes=VMEM_LIMIT),
        name="pair",
    )(pick, own, other)


def total(terms):
    while len(terms) > 1:
        terms = [terms[i] + terms[i + 1] for i in range(0, len(terms), 2)]
    return terms[0]


def eliminated(panel, at, j):
    sub = iota((8, RANK), 0)
    lane = iota((8, RANK), 1)
    inside = (lane >= at) & (lane < at + 8)

    def along(block, k):
        return jnp.take_along_axis(block, jnp.full((8, RANK), at + k, jnp.int32), axis=1)

    columns = [along(panel[j], k) for k in range(8)]
    block = jnp.where(inside, jnp.where(lane - at == sub, 1.0, 0.0), panel[j])
    for i in range(8):
        here = sub == i
        scale = 1.0 / columns[i][i : i + 1, :]
        factor = jnp.where(here, scale, -columns[i] * scale)

        def reduced(value):
            return jnp.where(here, 0.0, value) + factor * value[i : i + 1, :]

        block = reduced(block)
        columns = columns[: i + 1] + [reduced(column) for column in columns[i + 1 :]]
    return [
        block
        if m == j
        else jnp.where(inside, 0.0, panel[m]) - total([along(panel[m], k) * block[k : k + 1, :] for k in range(8)])
        for m in range(len(panel))
    ]


def inverses(grams, width):
    wide_lane = iota((width, RANK), 1)
    count, panels = width // 8, RANK // width
    matrices = [[gram[8 * m : 8 * m + 8, :] for m in range(RANK // 8)] for gram in grams]
    for p in range(panels):
        base = p * width
        inside = (wide_lane >= base) & (wide_lane < base + width)
        for matrix in matrices:
            panel = matrix[p * count : (p + 1) * count]
            for j in range(count):
                panel = eliminated(panel, base + 8 * j, j)
            rows = jnp.concatenate(panel, 0)
            for q in [(p + 1 + t) % panels for t in range(panels - 1)]:
                old = jnp.concatenate(matrix[q * count : (q + 1) * count], 0)
                new = jnp.where(inside, 0.0, old) - dot(old[:, base : base + width], rows, precision=HIGHEST)
                matrix[q * count : (q + 1) * count] = [new[8 * j : 8 * j + 8, :] for j in range(count)]
            matrix[p * count : (p + 1) * count] = panel
    return [jnp.concatenate(matrix, 0) for matrix in matrices]


def invert_between(ref, first, last, width):
    lane = iota((RANK, RANK), 1)
    count = width // 8

    def step(p, carry):
        base = pl.multiple_of(p * width, width)
        panel = [ref[pl.ds(base + 8 * j, 8), :] for j in range(count)]
        for j in range(count):
            panel = eliminated(panel, base + 8 * j, j)
        whole_matrix = ref[...]
        left = pltpu.roll(whole_matrix, RANK - base, 1)[:, :width]
        kept = jnp.where((lane >= base) & (lane < base + width), 0.0, whole_matrix)
        ref[...] = kept - dot(left, jnp.concatenate(panel, 0), precision=HIGHEST)
        for j in range(count):
            ref[pl.ds(base + 8 * j, 8), :] = panel[j]
        return carry

    lax.fori_loop(first, last, step, 0)


def half_rows(where_ref, upper_ref):
    half = RANK // 2
    return upper_ref[pl.ds(pl.multiple_of((where_ref[0] & 1) * half, half), half), :]


def interp_kernel(
    where_ref, leaf_gram_ref, leaf_cross_ref, chosen_ref, upper_ref, pick_ref,
    leaf_out, merge_out, mine_out, inverse_out, part_out, count_out,
):
    upper = upper_ref[...]
    pick = pick_ref[:, :RANK]
    mine = picked(pick, upper)
    mine_out[...] = mine
    taken = jnp.sum(pick.astype(F32), 1, keepdims=True)
    count_out[0] = jnp.sum(taken).astype(jnp.int32)
    diagonal = iota((RANK, RANK), 0) == iota((RANK, RANK), 1)
    others = jnp.where(diagonal, 1.0 - taken, 0.0)
    leaf_inverse, merge_inverse, mine_inverse = inverses(
        [leaf_gram_ref[...], dot(upper, upper, ROW_ROW, HIGHEST), dot(mine, mine, ROW_ROW, HIGHEST) + others], 32
    )
    inverse_out[...] = mine_inverse - others
    merge_cross = dot(chosen_ref[...], upper, ROW_ROW, HIGHEST)
    half = half_rows(where_ref, upper_ref)
    part_out[...] = dot(dot(half, mine, ROW_ROW, HIGHEST), mine_inverse - others, precision=HIGHEST)
    leaf_out[...] = dot(leaf_cross_ref[...], leaf_inverse, precision=HIGHEST)
    merge_out[...] = dot(merge_cross, merge_inverse, precision=HIGHEST)


def interp(where, leaf_gram, leaf_cross, chosen, upper, pick):
    return pl.pallas_call(
        interp_kernel,
        out_shape=[
            jax.ShapeDtypeStruct(leaf_cross.shape, F32),
            jax.ShapeDtypeStruct((RANK, RANK), F32),
            jax.ShapeDtypeStruct(upper.shape, F32),
            jax.ShapeDtypeStruct((RANK, RANK), F32),
            jax.ShapeDtypeStruct((RANK // 2, RANK), F32),
            jax.ShapeDtypeStruct((1,), jnp.int32),
        ],
        in_specs=[pl.BlockSpec(memory_space=pltpu.SMEM)] + [pl.BlockSpec(memory_space=pltpu.VMEM)] * 5,
        out_specs=[pl.BlockSpec(memory_space=pltpu.VMEM)] * 5 + [pl.BlockSpec(memory_space=pltpu.SMEM)],
        cost_estimate=pl.CostEstimate(flops=8_000_000_000, bytes_accessed=2_000_000, transcendentals=0),
        compiler_params=pltpu.CompilerParams(vmem_limit_bytes=VMEM_LIMIT),
        name="interp",
    )(where, leaf_gram, leaf_cross, chosen, upper, pick)


def top_kernel(
    where_ref, count_ref, pick_ref, upper_ref, across_ref, mine_ref, inverse_ref, part_ref,
    top_out, rows_out, rest, quad,
):
    position, width = where_ref[0], 16
    pick = pick_ref[:, RANK:]
    theirs = picked(pick, across_ref[...])
    mine, inverse, part = mine_ref[...], inverse_ref[...], part_ref[...]
    quad[...] = mine + theirs
    columns = pl.ds(pl.multiple_of(where_ref[1] * 128, 128), 128)
    rows_out[...] = quad[pl.ds(pl.multiple_of((position & 3) * (RANK // 4), RANK // 4), RANK // 4), columns]
    mixed = dot(mine, theirs, ROW_ROW, HIGHEST)
    passed = dot(inverse, mixed, precision=HIGHEST)
    taken = jnp.sum(pick.astype(F32), 1, keepdims=True)
    diagonal = iota((RANK, RANK), 0) == iota((RANK, RANK), 1)
    rest[...] = (
        dot(theirs, theirs, ROW_ROW, HIGHEST)
        - dot(mixed, passed, COL_COL, HIGHEST)
        + jnp.where(diagonal, 1.0 - taken, 0.0)
    )
    half = half_rows(where_ref, upper_ref)
    cross = dot(half, theirs, ROW_ROW, HIGHEST) - dot(part, mixed, precision=HIGHEST)
    own_count = count_ref[0]
    own_first = (lax.shift_right_arithmetic(position, 1) & 1) == 0
    begin = jnp.where(own_first, own_count, 0)
    end = jnp.where(own_first, RANK, RANK - own_count)
    invert_between(
        rest, lax.shift_right_arithmetic(begin, 4), lax.shift_right_arithmetic(end + width - 1, 4), width
    )
    side = dot(cross, rest[...], precision=HIGHEST)
    top_out[...] = part + side - dot(side, passed, ROW_ROW, HIGHEST)


def top(where, count, pick, upper, across, mine, inverse, part):
    return pl.pallas_call(
        top_kernel,
        out_shape=[jax.ShapeDtypeStruct((RANK // 2, RANK), F32), jax.ShapeDtypeStruct((RANK // 4, 128), F32)],
        in_specs=[pl.BlockSpec(memory_space=pltpu.SMEM)] * 2 + [pl.BlockSpec(memory_space=pltpu.VMEM)] * 6,
        out_specs=[pl.BlockSpec(memory_space=pltpu.VMEM)] * 2,
        scratch_shapes=[pltpu.VMEM((RANK, RANK), F32), pltpu.VMEM(upper.shape, F32)],
        compiler_params=pltpu.CompilerParams(vmem_limit_bytes=VMEM_LIMIT),
        name="top",
    )(where, count, pick, upper, across, mine, inverse, part)


def shifted(value, axis, steps):
    count = lax.axis_size(axis)
    first, last = (max(0, -steps), min(count, count - steps))
    return lax.ppermute(value, axis, [(source, source + steps) for source in range(first, last)])


def swapped(block, axis, apart):
    count = lax.axis_size(axis)
    return lax.ppermute(block, axis, [(i, i ^ (1 << apart)) for i in range(count)])


def crossed(block, axis, width):
    count = lax.axis_size(axis)
    up = [(i, i + width) for i in range(count - width) if i // width % 2 == 1]
    return lax.ppermute(block, axis, up + [(high, low) for low, high in up])


def body(
    probe, shift_real, shift_imag, child_gen, child_coef, child_map, child_of, leaf_skel, pair_skel, quad_skel
):
    row_count, _, col_count = probe.shape
    devices = lax.axis_size("row")
    where = jnp.stack([lax.axis_index("row"), lax.axis_index("samp")]).astype(jnp.int32)
    offset = LINE // row_count
    everyone = lax.all_gather(
        jnp.concatenate([probe.reshape(-1, col_count), child_coef.reshape(-1, col_count)], 0), "samp"
    )
    wide, coef = everyone[:, : 2 * row_count], everyone[:, 2 * row_count :]
    outgoing = route(child_map, child_of, child_gen, devices)
    got = lax.all_to_all(
        outgoing.reshape(devices * SLOT // 2, 2, -1), "row", split_axis=0, concat_axis=0, tiled=True
    ).reshape(devices * SLOT, -1)
    high = crossed(wide, "row", offset)
    low = swapped(wide, "row", 1)
    left = shifted(wide[:, -2:], "row", 1)
    right = shifted(wide[:, :2], "row", -1)
    base, leaf_pick, pair_pick, quad_pick = child(
        where, got, coef, wide, shift_real.reshape(-1, 128), shift_imag.reshape(-1, 128),
        leaf_skel, pair_skel, quad_skel,
    )
    own, leaf_rows, chosen = leaf(where, base, low, high, left, right, leaf_pick)
    leaf_gram, leaf_cross = products(leaf_rows, chosen)
    upper = pair(pair_pick, chosen, swapped(chosen, "row", 0))
    leaf_interp, merge_interp, mine, inverse, part, count = interp(
        where, leaf_gram, leaf_cross, chosen, upper, quad_pick
    )
    top_interp, top_rows = top(where, count, quad_pick, upper, swapped(upper, "row", 1), mine, inverse, part)
    return own.reshape(row_count, 2, col_count), leaf_interp, merge_interp, top_interp, top_rows


def solution(mesh):
    return jax.shard_map(
        body,
        mesh=mesh,
        in_specs=(
            P("row", None, "samp"),
            P("row"),
            P("row"),
            P("row", None),
            P(None, None, "samp"),
            P("row", None),
            P("row"),
            P("row", None),
            P(),
            P(),
        ),
        out_specs=(
            P("row", None, "samp"),
            P("row", None),
            P("row", None),
            P("row", None),
            P("row", "samp"),
        ),
        check_vma=False,
    )
```

```python
import functools

import jax
import jax.numpy as jnp
from jax import lax
from jax.experimental import pallas as pl
from jax.experimental.pallas import tpu as pltpu
from jax.sharding import PartitionSpec as P

LINE = 512
CAP = 8
SLOT = CAP + 2
RANK = 128
ROWS = 256
HIGHEST = lax.Precision.HIGHEST
F32 = jnp.float32
BF16 = jnp.bfloat16
VMEM_LIMIT = 24 * 1024 * 1024
VMEM_ALL = 60 * 1024 * 1024


def whole(value):
    return pl.BlockSpec(value.shape, lambda: (0,) * value.ndim)


def iota(shape, dim):
    return lax.broadcasted_iota(jnp.int32, shape, dim)


def column_of(row):
    square = jnp.broadcast_to(row, (128, 128))
    return jnp.sum(jnp.where(iota((128, 128), 0) == iota((128, 128), 1), square, jnp.zeros_like(square)), 1, keepdims=True)


def mask(condition):
    return jnp.where(condition, 1.0, 0.0).astype(BF16)


def picked(pick, rows):
    first = rows.astype(BF16)
    rest = rows - first.astype(F32)
    second = rest.astype(BF16)
    third = (rest - second.astype(F32)).astype(BF16)
    return dot(pick, first) + dot(pick, second) + dot(pick, third)


def side_by_side(ref):
    return jnp.concatenate([ref[s] for s in range(ref.shape[0])], 1)


def dot(a, b, dims=(((1,), (0,)), ((), ())), precision=None):
    return lax.dot_general(a, b, dims, precision=precision, preferred_element_type=F32)


ROW_ROW = (((1,), (1,)), ((), ()))
COL_COL = (((0,), (0,)), ((), ()))


def route_kernel(of_ref, map_ref, gen_ref, out_ref):
    blocks = map_ref.shape[0]
    count = blocks * 128
    targets = map_ref[...]
    owner = lax.shift_right_arithmetic(targets, 8)
    place = (targets & (ROWS - 1)) + 1
    owner_row = jnp.concatenate([owner[b : b + 1] for b in range(blocks)], 1).astype(F32)
    owner_col = jnp.concatenate([column_of(owner[b : b + 1].astype(F32)) for b in range(blocks)], 0)
    place_col = jnp.concatenate([column_of(place[b : b + 1].astype(F32)) for b in range(blocks)], 0)
    label_col = jnp.concatenate([jnp.full((128, 1), of_ref[b], jnp.int32) for b in range(blocks)], 0).astype(F32)
    same = jnp.where(owner_col == owner_row, 1.0, 0.0)
    sub, lane = iota((count, count), 0), iota((count, count), 1)
    within_row = jnp.sum(jnp.where(sub < lane, same, 0.0), 0, keepdims=True)
    within_col = jnp.sum(jnp.where(lane < sub, same, 0.0), 1, keepdims=True)
    slot_row = jnp.where(owner_row >= 0, owner_row * SLOT + within_row, -1.0).astype(jnp.int32)
    lanes = iota((count, 128), 1)
    within_at = within_col.astype(jnp.int32)
    info = jnp.where(lanes == within_at, place_col, 0.0) + jnp.where(lanes == within_at + CAP, label_col, 0.0)
    owns = mask(iota((RANK, count), 0) == owner_row.astype(jnp.int32))
    table = jnp.concatenate([gen_ref[...], dot(owns, info.astype(BF16)).astype(BF16)], 0)
    rows = out_ref.shape[0]
    info_row = iota((1, RANK), 1) * SLOT + CAP
    source_row = jnp.concatenate([slot_row, info_row], 1)
    step = min(256, rows)
    for first in range(0, rows, step):
        pick = mask(iota((step, count + RANK), 0) + first == source_row)
        out_ref[first : first + step] = dot(pick, table).astype(BF16)


def route(child_map, child_of, child_gen, devices):
    return pl.pallas_call(
        route_kernel,
        out_shape=jax.ShapeDtypeStruct((devices * SLOT, child_gen.shape[1]), BF16),
        in_specs=[pl.BlockSpec(memory_space=pltpu.SMEM), whole(child_map), whole(child_gen)],
        out_specs=pl.BlockSpec(memory_space=pltpu.VMEM),
        compiler_params=pltpu.CompilerParams(vmem_limit_bytes=VMEM_ALL),
        name="route",
    )(child_of, child_map, child_gen)


def one_hot(skel_ref, group, width, shift=0):
    picks = column_of(skel_ref[pl.ds(group, 1), :].astype(F32)).astype(jnp.int32)
    return mask(iota((RANK, width), 1) == ((picks + shift) & (width - 1)))


def child_kernel(
    where_ref, got_ref, coef_ref, x_ref, real_ref, imag_ref, leaf_skel_ref, pair_skel_ref, quad_skel_ref,
    out_ref, leaf_pick_ref, pair_pick_ref, quad_pick_ref,
):
    position = where_ref[0]
    low, high = position & 1, lax.shift_right_arithmetic(position, 1) & 1
    leaf_pick_ref[...] = one_hot(leaf_skel_ref, 0, 2 * ROWS)
    pair_pick_ref[...] = one_hot(pair_skel_ref, lax.shift_right_arithmetic(position, 1), 2 * RANK, RANK * low)
    quad_pick_ref[...] = one_hot(quad_skel_ref, lax.shift_right_arithmetic(position, 2), 2 * RANK, RANK * high)
    rows = 2 * ROWS
    sub_x = iota((rows, 128), 0)
    half = lax.shift_right_arithmetic(iota((256, 128), 0), 1) == iota((256, 128), 1)

    def spread_rows(ref):
        blocks = [jnp.sum(jnp.where(half, ref[b : b + 1, :], 0.0), 1, keepdims=True) for b in range(ref.shape[0])]
        return jnp.concatenate(blocks, 0)

    real, imag = spread_rows(real_ref) + 4.0, spread_rows(imag_ref)
    got = got_ref[...]
    count = got.shape[0]
    sources = count // SLOT
    info_at = iota((sources, count), 0) * SLOT + CAP == iota((sources, count), 1)
    info = dot(jnp.where(info_at, 1.0, 0.0).astype(BF16), got).astype(BF16)
    along = iota((count, sources), 0)
    source = lax.shift_right_arithmetic(along * 6554, 16)
    spread = dot(jnp.where(source == iota((count, sources), 1), 1.0, 0.0).astype(BF16), info)
    sub = iota((count, 128), 0)
    slot = sub - SLOT * lax.shift_right_arithmetic(sub * 6554, 16)
    ones = jnp.full((128, 128), 1.0, BF16)
    label = dot(jnp.where(iota((count, 128), 1) == slot + CAP, spread, 0.0).astype(BF16), ones)
    along_t = iota((sources, count), 1)
    source_t = lax.shift_right_arithmetic(along_t * 6554, 16)
    spread_t = dot(info, jnp.where(source_t == iota((sources, count), 0), 1.0, 0.0).astype(BF16), COL_COL)
    lane = iota((128, count), 1)
    slot_t = lane - SLOT * lax.shift_right_arithmetic(lane * 6554, 16)
    sub_t = iota((128, count), 0)
    code = jnp.sum(jnp.where((sub_t == slot_t) & (sub_t < CAP), spread_t, 0.0), 0, keepdims=True)
    onto = jnp.where(iota((ROWS, count), 0) + 1 == code.astype(jnp.int32), 1.0, 0.0).astype(BF16)
    second = got * label.astype(BF16)
    parts = jnp.concatenate([got - second, second], 1)
    rank = coef_ref.shape[1] // 2
    for s in range(coef_ref.shape[0]):
        coef = coef_ref[s]
        first, second, none = coef[:rank], coef[rank:], jnp.zeros((rank, 128), BF16)
        table = jnp.concatenate(
            [jnp.concatenate([first, none, second, none], 0), jnp.concatenate([none, first, none, second], 0)], 1
        )
        values = dot(parts, table).astype(BF16)
        sums = dot(onto, values)
        for c in range(2):
            out_ref[s, pl.ds(c, ROWS, stride=2), :] = sums[:, c * 128 : (c + 1) * 128]
        x = x_ref[s].astype(F32)
        before = jnp.where(sub_x < 2, 0.0, pltpu.roll(x, 2, 0))
        after = jnp.where(sub_x >= rows - 2, 0.0, pltpu.roll(x, rows - 2, 0))
        turned = jnp.where((sub_x & 1) == 0, -pltpu.roll(x, rows - 1, 0), pltpu.roll(x, 1, 0))
        out_ref[s] = out_ref[s] + (real * x + imag * turned - (before + after))


def child(where, got, coef, x, *others):
    return pl.pallas_call(
        child_kernel,
        out_shape=[
            jax.ShapeDtypeStruct((coef.shape[0], 2 * ROWS, coef.shape[2]), F32),
            jax.ShapeDtypeStruct((RANK, 2 * ROWS), BF16),
            jax.ShapeDtypeStruct((RANK, 2 * RANK), BF16),
            jax.ShapeDtypeStruct((RANK, 2 * RANK), BF16),
        ],
        in_specs=[pl.BlockSpec(memory_space=pltpu.SMEM)]
        + [pl.BlockSpec(memory_space=pltpu.VMEM)] * 3
        + [whole(value) for value in others],
        out_specs=[pl.BlockSpec(memory_space=pltpu.VMEM)] * 4,
        cost_estimate=pl.CostEstimate(flops=2_000_000_000, bytes_accessed=2_000_000, transcendentals=0),
        compiler_params=pltpu.CompilerParams(vmem_limit_bytes=VMEM_LIMIT),
        name="child",
    )(where, got, coef, x, *others)


def leaf_kernel(where_ref, part_ref, low_ref, high_ref, left_ref, right_ref, pick_ref, leaf_ref, chosen_ref):
    parts, rows, width = part_ref.shape
    sub = iota((8, width), 0)
    for s in range(parts):
        left, right = left_ref[s].astype(F32), right_ref[s].astype(F32)
        leaf_ref[s] = part_ref[s] - (low_ref[s].astype(F32) + high_ref[s].astype(F32))
        first = jnp.where(sub == 0, left[0:1], jnp.where(sub == 1, left[1:2], 0.0))
        last = jnp.where(sub == 6, right[0:1], jnp.where(sub == 7, right[1:2], 0.0))
        leaf_ref[s, 0:8, :] = leaf_ref[s, 0:8, :] - first
        leaf_ref[s, rows - 8 : rows, :] = leaf_ref[s, rows - 8 : rows, :] - last
    chosen_ref[...] = picked(pick_ref[...], side_by_side(leaf_ref))


def leaf(where, part, *others):
    parts, rows, width = part.shape
    return pl.pallas_call(
        leaf_kernel,
        out_shape=[
            jax.ShapeDtypeStruct(part.shape, F32),
            jax.ShapeDtypeStruct((RANK, parts * width), F32),
        ],
        in_specs=[pl.BlockSpec(memory_space=pltpu.SMEM)] + [pl.BlockSpec(memory_space=pltpu.VMEM)] * 6,
        out_specs=[pl.BlockSpec(memory_space=pltpu.VMEM)] * 2,
        compiler_params=pltpu.CompilerParams(vmem_limit_bytes=VMEM_LIMIT),
        name="leaf",
    )(where, part, *others)


def products_kernel(leaf_ref, chosen_ref, gram_ref, cross_ref):
    chosen = chosen_ref[...]
    gram_ref[...] = dot(chosen, chosen, ROW_ROW, HIGHEST)
    cross_ref[...] = dot(side_by_side(leaf_ref), chosen, ROW_ROW, HIGHEST)


def products(leaf_rows, chosen):
    return pl.pallas_call(
        products_kernel,
        out_shape=[
            jax.ShapeDtypeStruct((RANK, RANK), F32),
            jax.ShapeDtypeStruct((leaf_rows.shape[1], RANK), F32),
        ],
        in_specs=[pl.BlockSpec(memory_space=pltpu.VMEM)] * 2,
        out_specs=[pl.BlockSpec(memory_space=pltpu.VMEM)] * 2,
        cost_estimate=pl.CostEstimate(flops=1_000_000_000, bytes_accessed=2_000_000, transcendentals=0),
        compiler_params=pltpu.CompilerParams(vmem_limit_bytes=VMEM_LIMIT),
        name="products",
    )(leaf_rows, chosen)


def pair_kernel(pick_ref, own_ref, other_ref, out_ref):
    out_ref[...] = picked(pick_ref[...], jnp.concatenate([own_ref[...], other_ref[...]], 0))


def pair(pick, own, other):
    return pl.pallas_call(
        pair_kernel,
        out_shape=jax.ShapeDtypeStruct(own.shape, F32),
        in_specs=[pl.BlockSpec(memory_space=pltpu.VMEM)] * 3,
        out_specs=pl.BlockSpec(memory_space=pltpu.VMEM),
        compiler_params=pltpu.CompilerParams(vmem_limit_bytes=VMEM_LIMIT),
        name="pair",
    )(pick, own, other)


def total(terms):
    while len(terms) > 1:
        terms = [terms[i] + terms[i + 1] for i in range(0, len(terms), 2)]
    return terms[0]


def eliminated(panel, at, j):
    sub = iota((8, RANK), 0)
    lane = iota((8, RANK), 1)
    inside = (lane >= at) & (lane < at + 8)

    def along(block, k):
        return jnp.take_along_axis(block, jnp.full((8, RANK), at + k, jnp.int32), axis=1)

    columns = [along(panel[j], k) for k in range(8)]
    block = jnp.where(inside, jnp.where(lane - at == sub, 1.0, 0.0), panel[j])
    for i in range(8):
        here = sub == i
        scale = 1.0 / columns[i][i : i + 1, :]
        factor = jnp.where(here, scale, -columns[i] * scale)

        def reduced(value):
            return jnp.where(here, 0.0, value) + factor * value[i : i + 1, :]

        block = reduced(block)
        columns = columns[: i + 1] + [reduced(column) for column in columns[i + 1 :]]
    return [
        block
        if m == j
        else jnp.where(inside, 0.0, panel[m]) - total([along(panel[m], k) * block[k : k + 1, :] for k in range(8)])
        for m in range(len(panel))
    ]


def inverses(grams, width):
    wide_lane = iota((width, RANK), 1)
    count, panels = width // 8, RANK // width
    matrices = [[gram[8 * m : 8 * m + 8, :] for m in range(RANK // 8)] for gram in grams]
    for p in range(panels):
        base = p * width
        inside = (wide_lane >= base) & (wide_lane < base + width)
        for matrix in matrices:
            panel = matrix[p * count : (p + 1) * count]
            for j in range(count):
                panel = eliminated(panel, base + 8 * j, j)
            rows = jnp.concatenate(panel, 0)
            for q in [(p + 1 + t) % panels for t in range(panels - 1)]:
                old = jnp.concatenate(matrix[q * count : (q + 1) * count], 0)
                new = jnp.where(inside, 0.0, old) - dot(old[:, base : base + width], rows, precision=HIGHEST)
                matrix[q * count : (q + 1) * count] = [new[8 * j : 8 * j + 8, :] for j in range(count)]
            matrix[p * count : (p + 1) * count] = panel
    return [jnp.concatenate(matrix, 0) for matrix in matrices]


def invert_between(ref, first, last, width):
    lane = iota((RANK, RANK), 1)
    count = width // 8

    def step(p, carry):
        base = pl.multiple_of(p * width, width)
        panel = [ref[pl.ds(base + 8 * j, 8), :] for j in range(count)]
        for j in range(count):
            panel = eliminated(panel, base + 8 * j, j)
        whole_matrix = ref[...]
        left = pltpu.roll(whole_matrix, RANK - base, 1)[:, :width]
        kept = jnp.where((lane >= base) & (lane < base + width), 0.0, whole_matrix)
        ref[...] = kept - dot(left, jnp.concatenate(panel, 0), precision=HIGHEST)
        for j in range(count):
            ref[pl.ds(base + 8 * j, 8), :] = panel[j]
        return carry

    lax.fori_loop(first, last, step, 0)


def half_rows(where_ref, upper_ref):
    half = RANK // 2
    return upper_ref[pl.ds(pl.multiple_of((where_ref[0] & 1) * half, half), half), :]


def interp_kernel(
    where_ref, leaf_ref, leaf_gram_ref, leaf_cross_ref, chosen_ref, upper_ref, pick_ref,
    own_out, leaf_out, merge_out, mine_out, inverse_out, part_out, count_out, own_sem,
):
    leave = pltpu.make_async_copy(leaf_ref.at[where_ref[1]], own_out, own_sem)
    leave.start()
    upper = upper_ref[...]
    pick = pick_ref[:, :RANK]
    mine = picked(pick, upper)
    mine_out[...] = mine
    taken = jnp.sum(pick.astype(F32), 1, keepdims=True)
    count_out[0] = jnp.sum(taken).astype(jnp.int32)
    diagonal = iota((RANK, RANK), 0) == iota((RANK, RANK), 1)
    others = jnp.where(diagonal, 1.0 - taken, 0.0)
    leaf_inverse, merge_inverse, mine_inverse = inverses(
        [leaf_gram_ref[...], dot(upper, upper, ROW_ROW, HIGHEST), dot(mine, mine, ROW_ROW, HIGHEST) + others], 32
    )
    inverse_out[...] = mine_inverse - others
    merge_cross = dot(chosen_ref[...], upper, ROW_ROW, HIGHEST)
    half = half_rows(where_ref, upper_ref)
    part_out[...] = dot(dot(half, mine, ROW_ROW, HIGHEST), mine_inverse - others, precision=HIGHEST)
    leaf_out[...] = dot(leaf_cross_ref[...], leaf_inverse, precision=HIGHEST)
    merge_out[...] = dot(merge_cross, merge_inverse, precision=HIGHEST)
    leave.wait()


def interp(where, leaf_rows, leaf_gram, leaf_cross, chosen, upper, pick):
    return pl.pallas_call(
        interp_kernel,
        out_shape=[
            jax.ShapeDtypeStruct(leaf_rows.shape[1:], F32),
            jax.ShapeDtypeStruct(leaf_cross.shape, F32),
            jax.ShapeDtypeStruct((RANK, RANK), F32),
            jax.ShapeDtypeStruct(upper.shape, F32),
            jax.ShapeDtypeStruct((RANK, RANK), F32),
            jax.ShapeDtypeStruct((RANK // 2, RANK), F32),
            jax.ShapeDtypeStruct((1,), jnp.int32),
        ],
        in_specs=[pl.BlockSpec(memory_space=pltpu.SMEM)] + [pl.BlockSpec(memory_space=pltpu.VMEM)] * 6,
        out_specs=[pl.BlockSpec(memory_space=pl.ANY)]
        + [pl.BlockSpec(memory_space=pltpu.VMEM)] * 5
        + [pl.BlockSpec(memory_space=pltpu.SMEM)],
        scratch_shapes=[pltpu.SemaphoreType.DMA],
        cost_estimate=pl.CostEstimate(flops=8_000_000_000, bytes_accessed=2_000_000, transcendentals=0),
        compiler_params=pltpu.CompilerParams(vmem_limit_bytes=VMEM_LIMIT),
        name="interp",
    )(where, leaf_rows, leaf_gram, leaf_cross, chosen, upper, pick)


def top_kernel(
    where_ref, count_ref, pick_ref, upper_ref, across_ref, mine_ref, inverse_ref, part_ref,
    top_out, rows_out, rest, quad,
):
    position, width = where_ref[0], 16
    pick = pick_ref[:, RANK:]
    theirs = picked(pick, across_ref[...])
    mine, inverse, part = mine_ref[...], inverse_ref[...], part_ref[...]
    quad[...] = mine + theirs
    columns = pl.ds(pl.multiple_of(where_ref[1] * 128, 128), 128)
    rows_out[...] = quad[pl.ds(pl.multiple_of((position & 3) * (RANK // 4), RANK // 4), RANK // 4), columns]
    mixed = dot(mine, theirs, ROW_ROW, HIGHEST)
    passed = dot(inverse, mixed, precision=HIGHEST)
    taken = jnp.sum(pick.astype(F32), 1, keepdims=True)
    diagonal = iota((RANK, RANK), 0) == iota((RANK, RANK), 1)
    rest[...] = (
        dot(theirs, theirs, ROW_ROW, HIGHEST)
        - dot(mixed, passed, COL_COL, HIGHEST)
        + jnp.where(diagonal, 1.0 - taken, 0.0)
    )
    half = half_rows(where_ref, upper_ref)
    cross = dot(half, theirs, ROW_ROW, HIGHEST) - dot(part, mixed, precision=HIGHEST)
    own_count = count_ref[0]
    own_first = (lax.shift_right_arithmetic(position, 1) & 1) == 0
    begin = jnp.where(own_first, own_count, 0)
    end = jnp.where(own_first, RANK, RANK - own_count)
    invert_between(
        rest, lax.shift_right_arithmetic(begin, 4), lax.shift_right_arithmetic(end + width - 1, 4), width
    )
    side = dot(cross, rest[...], precision=HIGHEST)
    top_out[...] = part + side - dot(side, passed, ROW_ROW, HIGHEST)


def top(where, count, pick, upper, across, mine, inverse, part):
    return pl.pallas_call(
        top_kernel,
        out_shape=[jax.ShapeDtypeStruct((RANK // 2, RANK), F32), jax.ShapeDtypeStruct((RANK // 4, 128), F32)],
        in_specs=[pl.BlockSpec(memory_space=pltpu.SMEM)] * 2 + [pl.BlockSpec(memory_space=pltpu.VMEM)] * 6,
        out_specs=[pl.BlockSpec(memory_space=pltpu.VMEM)] * 2,
        scratch_shapes=[pltpu.VMEM((RANK, RANK), F32), pltpu.VMEM(upper.shape, F32)],
        compiler_params=pltpu.CompilerParams(vmem_limit_bytes=VMEM_LIMIT),
        name="top",
    )(where, count, pick, upper, across, mine, inverse, part)


def shifted(value, axis, steps):
    count = lax.axis_size(axis)
    first, last = (max(0, -steps), min(count, count - steps))
    return lax.ppermute(value, axis, [(source, source + steps) for source in range(first, last)])


def swapped(block, axis, apart):
    count = lax.axis_size(axis)
    return lax.ppermute(block, axis, [(i, i ^ (1 << apart)) for i in range(count)])


def crossed(block, axis, width):
    count = lax.axis_size(axis)
    up = [(i, i + width) for i in range(count - width) if i // width % 2 == 1]
    return lax.ppermute(block, axis, up + [(high, low) for low, high in up])


def body(
    probe, shift_real, shift_imag, child_gen, child_coef, child_map, child_of, leaf_skel, pair_skel, quad_skel
):
    row_count, _, col_count = probe.shape
    devices = lax.axis_size("row")
    where = jnp.stack([lax.axis_index("row"), lax.axis_index("samp")]).astype(jnp.int32)
    offset = LINE // row_count
    everyone = lax.all_gather(
        jnp.concatenate([probe.reshape(-1, col_count), child_coef.reshape(-1, col_count)], 0), "samp"
    )
    wide, coef = everyone[:, : 2 * row_count], everyone[:, 2 * row_count :]
    outgoing = route(child_map, child_of, child_gen, devices)
    got = lax.all_to_all(
        outgoing.reshape(devices * SLOT // 2, 2, -1), "row", split_axis=0, concat_axis=0, tiled=True
    ).reshape(devices * SLOT, -1)
    high = crossed(wide, "row", offset)
    low = swapped(wide, "row", 1)
    left = shifted(wide[:, -2:], "row", 1)
    right = shifted(wide[:, :2], "row", -1)
    base, leaf_pick, pair_pick, quad_pick = child(
        where, got, coef, wide, shift_real.reshape(-1, 128), shift_imag.reshape(-1, 128),
        leaf_skel, pair_skel, quad_skel,
    )
    leaf_rows, chosen = leaf(where, base, low, high, left, right, leaf_pick)
    leaf_gram, leaf_cross = products(leaf_rows, chosen)
    upper = pair(pair_pick, chosen, swapped(chosen, "row", 0))
    own, leaf_interp, merge_interp, mine, inverse, part, count = interp(
        where, leaf_rows, leaf_gram, leaf_cross, chosen, upper, quad_pick
    )
    top_interp, top_rows = top(where, count, quad_pick, upper, swapped(upper, "row", 1), mine, inverse, part)
    return own.reshape(row_count, 2, col_count), leaf_interp, merge_interp, top_interp, top_rows


def solution(mesh):
    return jax.shard_map(
        body,
        mesh=mesh,
        in_specs=(
            P("row", None, "samp"),
            P("row"),
            P("row"),
            P("row", None),
            P(None, None, "samp"),
            P("row", None),
            P("row"),
            P("row", None),
            P(),
            P(),
        ),
        out_specs=(
            P("row", None, "samp"),
            P("row", None),
            P("row", None),
            P("row", None),
            P("row", "samp"),
        ),
        check_vma=False,
    )
```
